128 devices in a mesh: blk: 64 (over y, z_lo, x, core), team: 2 (over z_hi).
Axes of the slice: x: 4, y: 4, z: 4 (z_hi: 2, z_lo: 2; z = z_hi * 2 + z_lo), core: 2. Of those that a mesh axis runs over, the one named last changes fastest.
Arguments:
- queries: bfloat16 [4096, 64, 128], P('blk'), may hold values from -6 to 6
- head_weights: float32 [4096, 64], P('blk'), may hold values from -0.75 to 0.75
- keys: bfloat16 [16384, 128], P('blk'), may hold values from -6 to 6
- query_pos: int32 [4096], P('blk'), may hold values from 0 to 16383
- block_limits: int32 [256], P('blk'), may hold values from 1 to 64
Outputs:
- block_logits: float32 [4096, 256], P('blk')
The draws below stay inside these ranges and needn't reach their ends.
All inputs are finite; a program needn't handle non-finite values.
Results may differ from the reference program's by a relative error of at most 0.0022.
Values may be sent and summed in bfloat16 or wider, within the bound.
No kernel may reach another device: no remote copies, remote signals or barrier semaphores. Data moves between devices by JAX's collectives and lax.ppermute only.
A program may use at most 64 MiB of HBM per device.

```python
import jax
import jax.numpy as jnp
from jax import lax

H = 64
HD = 128
BLOCK = 64
QUERIES = 4096
KEYS = 16384
NBLOCKS = 256


def with_ends(drawn, rng, low, high):
    longest = drawn.shape.index(max(drawn.shape))
    spots = []
    for shift in (0, 1):
        where = [jax.random.randint(jax.random.fold_in(rng, axis), (), 0, length) for axis, length in enumerate(drawn.shape)]
        where[longest] = (where[longest] + shift) % drawn.shape[longest]
        spots.append(tuple(where))
    return drawn.at[spots[0]].set(low).at[spots[1]].set(high)


def block_scale(own_key, extent, shards, low, high):
    def one(position, parts):
        steps = jax.random.uniform(jax.random.fold_in(jax.random.fold_in(own_key, 6), position), (parts,), jnp.float32, low / len(shards), high / len(shards))
        return jnp.repeat(jnp.exp(steps), extent[position] // parts).reshape((-1,) + (1,) * (len(extent) - position - 1))

    level = one(*shards[0])
    for cut in shards[1:]:
        level = level * one(*cut)
    return level


def centred(key, shape, deviation, most, cuts=(), kind=jnp.bfloat16):
    values = jax.random.normal(key, shape, jnp.float32) * deviation
    if len(cuts) > 0:
        values = block_scale(key, shape, cuts, -0.22, 0.18) * values
    return jnp.clip(values, min=-most, max=most).astype(kind)


def setup_inputs(seed: int = 0) -> dict:
    seeds = jax.random.split(jax.random.key(seed), 6)
    return {
        "queries": centred(seeds[0], (QUERIES, H, HD), 1.0, 6.0, ((0, 64),)),
        "head_weights": centred(seeds[1], (QUERIES, H), 0.125, 0.75, ((0, 64),), jnp.float32),
        "keys": centred(seeds[2], (KEYS, HD), 1.0, 6.0, ((0, 64),)),
        "query_pos": with_ends(jax.random.randint(seeds[3], (QUERIES,), 0, KEYS), jax.random.fold_in(seeds[3], 1), 0, KEYS - 1).astype(jnp.int32),
        "block_limits": with_ends(jax.random.randint(seeds[4], (NBLOCKS,), 1, BLOCK + 1), jax.random.fold_in(seeds[4], 1), 1, BLOCK).astype(jnp.int32),
    }


mask_value = -8.0


def reference(queries, head_weights, keys, query_pos, block_limits):
    key_index = jnp.arange(KEYS, dtype=jnp.int32)
    filled = (key_index % BLOCK) < jnp.repeat(block_limits, BLOCK)
    keys_wide = keys.astype(jnp.float32)
    scale = HD ** -0.5

    def one_group(args):
        query_rows, weight_rows, position_rows = args
        raw = jnp.einsum("chd,kd->chk", query_rows.astype(jnp.float32), keys_wide, precision=lax.Precision.HIGHEST)
        score = jnp.sum(jax.nn.relu(raw) * weight_rows[:, :, None], axis=1) * scale
        visible = filled[None, :] & (key_index[None, :] <= position_rows[:, None])
        masked = jnp.where(visible, score, mask_value)
        return jnp.max(masked.reshape(masked.shape[0], NBLOCKS, BLOCK), axis=-1)

    group = 8
    pooled = lax.map(one_group, (queries.reshape(QUERIES // group, group, H, HD), head_weights.reshape(QUERIES // group, group, H), query_pos.reshape(QUERIES // group, group)))
    return pooled.reshape(QUERIES, NBLOCKS)
```

```python
import jax
import jax.numpy as jnp
from jax import lax
from jax.experimental import pallas as pl
from jax.experimental.pallas import tpu as pltpu
from jax.sharding import PartitionSpec as P

BLOCK = 64
CHUNK = 16
GROUP = 16
TILE = 512
MARK = 100.0
FAR = 1 << 30
mask_value = -8.0


def swapped(value, pairs, axis):
    return lax.ppermute(value, axis, pairs)


def kernel(tokens, heads, rank_ref, sorted_ref, base_ref, own_ref, other_ref, weight_ref, key_ref,
           seen_ref, at_ref, unsort_ref, spread_ref, mine_ref, theirs_ref, q_ref, w_ref, max_ref):
    half = tokens // 2
    tiles = key_ref.shape[0] // TILE
    head_size = key_ref.shape[1]
    per_tile = TILE // BLOCK
    parts = BLOCK // CHUNK

    def arrange(token, _):
        for ref, first in ((own_ref, 0), (other_ref, half)):
            to = pl.multiple_of(rank_ref[first + token] * heads, heads)
            start = pl.multiple_of(token * heads, heads)
            q_ref[pl.ds(to, heads), :] = ref[pl.ds(start, heads), :]
            w_ref[pl.ds(to, heads), :] = weight_ref[pl.ds(pl.multiple_of((first + token) * heads, heads), heads), :]
        return 0

    lax.fori_loop(0, half, arrange, 0)
    max_ref[...] = jnp.full(max_ref.shape, mask_value, jnp.float32)

    def tile_step(tile, _):
        first = base_ref[0] + tile * (per_tile * 4 * BLOCK)
        groups = jnp.int32(0)
        for group in range(tokens // GROUP):
            groups = groups + (sorted_ref[group * GROUP] >= first).astype(jnp.int32)
        keys = jnp.concatenate(
            [
                key_ref[pl.ds(pl.multiple_of(tile * TILE + block * BLOCK + part * CHUNK, CHUNK), CHUNK), :]
                for part in range(parts)
                for block in range(per_tile)
            ],
            axis=0,
        )

        def group_step(group):
            row = pl.multiple_of(group * GROUP * heads, GROUP * heads)
            token = pl.multiple_of(group * GROUP, GROUP)
            raw = lax.dot_general(
                q_ref[pl.ds(row, GROUP * heads), :], keys, (((1,), (1,)), ((), ())), preferred_element_type=jnp.float32
            )
            weights = w_ref[pl.ds(row, GROUP * heads), :]
            at = at_ref[pl.ds(token, GROUP), :]
            best = None
            for part in range(parts):
                lanes = slice(part * 128, part * 128 + 128)
                terms = jnp.maximum(raw[:, lanes], 0.0) * weights
                score = terms.reshape(GROUP, heads // 8, 8, 128).sum(1).sum(1)
                seen = seen_ref[tile, 0:1, lanes]
                score = jnp.where(seen <= at, score, mask_value)
                best = score if best is None else jnp.maximum(best, score)
            max_ref[tile, pl.ds(token, GROUP), :] = best

        def pair_step(pair, _):
            group_step(2 * pair)
            group_step(2 * pair + 1)
            return 0

        lax.fori_loop(0, groups // 2, pair_step, 0)

        @pl.when(groups % 2 == 1)
        def _():
            group_step(groups - 1)

        return 0

    lax.fori_loop(0, tiles, tile_step, 0)
    lane = lax.broadcasted_iota(jnp.int32, (tokens, 128), 1)
    found = [max_ref[tile] for tile in range(tiles)]
    step = CHUNK // 2
    while step:
        low = (lane & step) == 0
        if len(found) > 1:
            found = [
                jnp.where(
                    low,
                    jnp.maximum(a, pltpu.roll(a, 128 - step, 1)),
                    jnp.maximum(b, pltpu.roll(b, step, 1)),
                )
                for a, b in zip(found[::2], found[1::2])
            ]
        else:
            found = [jnp.maximum(found[0], pltpu.roll(found[0], 128 - step, 1))]
        step //= 2
    pooled = found[0].astype(jnp.bfloat16)
    ordered = jnp.dot(unsort_ref[...], pooled, preferred_element_type=jnp.float32).astype(jnp.bfloat16)
    placed = jnp.dot(ordered, spread_ref[...], preferred_element_type=jnp.float32).astype(jnp.bfloat16)
    mine_ref[...] = placed[:half]
    theirs_ref[...] = placed[half:]


def body(queries, head_weights, keys, query_pos, block_limits):
    shards = lax.axis_size("blk")
    me = lax.axis_index("blk")
    core = me % 2
    member = lax.axis_index("team")
    quarter = 2 * member + core
    count, heads, head_size = queries.shape
    tokens = 2 * count
    local_blocks = keys.shape[0] // BLOCK
    cores = [(i, i ^ 1) for i in range(shards)]

    own = queries.reshape(count * heads, head_size)
    other = swapped(own, cores, "blk")
    positions = jnp.concatenate([query_pos, swapped(query_pos, cores, "blk")])
    weights = jnp.concatenate([head_weights, swapped(head_weights, cores, "blk")]) * head_size ** (-0.5)
    wide = jnp.broadcast_to(weights.reshape(tokens * heads, 1), (tokens * heads, 128))

    blocks = keys.reshape(local_blocks, BLOCK, head_size)
    row = lax.broadcasted_iota(jnp.int32, (local_blocks, BLOCK, 1), 1)
    limit = block_limits[:, None, None]
    blocks = jnp.where((row == BLOCK - 1) & (limit < BLOCK), (limit + MARK).astype(keys.dtype), blocks)
    keep = lax.dynamic_index_in_dim(blocks, quarter, 0, False)
    give = lax.dynamic_index_in_dim(blocks, quarter ^ 1, 0, False)
    got = swapped(give, cores, "blk")
    piece = jnp.where(core == 0, jnp.stack([keep, got]), jnp.stack([got, keep]))
    chips = shards // 2
    groups = [[2 * chip + c for chip in range(chips)] for c in range(2)]
    gathered = lax.all_to_all(
        jnp.broadcast_to(piece[None], (chips,) + piece.shape), "blk", 0, 0, axis_index_groups=groups
    )
    slab = gathered.reshape(shards, BLOCK, head_size)

    mark = slab[:, BLOCK - 1, 0].astype(jnp.float32)
    filled = jnp.where(mark > MARK / 2, mark - MARK, float(BLOCK)).astype(jnp.int32)
    tiles = shards * BLOCK // TILE
    per_tile = TILE // BLOCK
    shape = (tiles, BLOCK // CHUNK, per_tile, CHUNK)
    axis = lambda n: lax.broadcasted_iota(jnp.int32, shape, n)
    offset = axis(1) * CHUNK + axis(3)
    key_at = (axis(0) * per_tile + axis(2)) * (local_blocks * BLOCK) + quarter * BLOCK + offset
    seen = jnp.where(offset < filled.reshape(tiles, 1, per_tile, 1), key_at, FAR).reshape(tiles, 1, TILE)

    index = jnp.arange(tokens, dtype=jnp.int32)
    ahead = (positions[None, :] > positions[:, None]) | (
        (positions[None, :] == positions[:, None]) & (index[None, :] < index[:, None])
    )
    rank = jnp.sum(ahead.astype(jnp.int32), axis=1)
    hit = rank[None, :] == index[:, None]
    in_order = jnp.sum(jnp.where(hit, positions[None, :], 0), axis=1)
    at = jnp.broadcast_to(in_order[:, None], (tokens, 128))
    unsort = (rank[:, None] == index[None, :]).astype(jnp.bfloat16)
    lane = jnp.arange(128, dtype=jnp.int32)
    tile_of = ((lane >> 3) & 1) + 2 * ((lane >> 2) & 1) + 4 * ((lane >> 1) & 1)
    block_of = tile_of * per_tile + lane // CHUNK
    column = block_of * local_blocks + quarter
    spread = ((lane % 2 == 0)[:, None] & (column[:, None] == jnp.arange(shards * local_blocks)[None, :])).astype(jnp.bfloat16)

    smem = pl.BlockSpec(memory_space=pltpu.SMEM)
    vmem = pl.BlockSpec(memory_space=pltpu.VMEM)
    result = jax.ShapeDtypeStruct((count, shards * local_blocks), jnp.bfloat16)
    mine, theirs = pl.pallas_call(
        lambda *refs: kernel(tokens, heads, *refs),
        out_shape=(result, result),
        in_specs=[smem] * 3 + [vmem] * 8,
        out_specs=(vmem, vmem),
        scratch_shapes=[
            pltpu.VMEM((tokens * heads, head_size), jnp.bfloat16),
            pltpu.VMEM((tokens * heads, 128), jnp.float32),
            pltpu.VMEM((tiles, tokens, 128), jnp.float32),
        ],
        compiler_params=pltpu.CompilerParams(vmem_limit_bytes=40 * 2**20),
        name="pooled_scores",
    )(rank, in_order, (quarter * BLOCK)[None].astype(jnp.int32), own, other, wide, slab.reshape(-1, head_size), seen, at, unsort, spread)
    chip = mine + swapped(theirs, cores, "blk")
    return (chip + swapped(chip, [(0, 1), (1, 0)], "team")).astype(jnp.float32)


def solution(mesh):
    in_specs = (P("blk", None, None), P("blk", None), P("blk", None), P("blk"), P("blk"))
    out_specs = P("blk", None)
    return jax.shard_map(body, mesh=mesh, in_specs=in_specs, out_specs=out_specs, check_vma=False)
```

```python
import jax
import jax.numpy as jnp
from jax import lax
from jax.experimental import pallas as pl
from jax.experimental.pallas import tpu as pltpu
from jax.sharding import PartitionSpec as P

BLOCK = 64
CHUNK = 16
GROUP = 16
TILE = 256
PARTS = BLOCK // CHUNK
SLOTS = TILE // CHUNK
MARK = 100.0
SIDES = 4
STEPS = (0, 1, 3, 2)
FAR = 1 << 30
mask_value = -8.0


def swapped(value, pairs, axis):
    return lax.ppermute(value, axis, pairs)


def marked(limit_hbm, key_hbm, keep_ref, give_ref, limit_ref, sems):
    me = lax.axis_index("blk")
    keep = 2 * lax.axis_index("team") + me % 2
    picks = ((keep_ref, keep), (give_ref, keep + 1 - 2 * (keep % 2)))
    copies = [pltpu.make_async_copy(limit_hbm, limit_ref, sems.at[2])]
    for n, (ref, block) in enumerate(picks):
        start = pl.multiple_of(block * BLOCK, BLOCK)
        copies.append(pltpu.make_async_copy(key_hbm.at[pl.ds(start, BLOCK), :], ref, sems.at[n]))
    for copy in copies:
        copy.start()
    for copy in copies:
        copy.wait()
    for ref, block in picks:
        limit = limit_ref[block]
        last = ref[BLOCK - CHUNK:, :].astype(jnp.float32)
        row = lax.broadcasted_iota(jnp.int32, last.shape, 0)
        column = lax.broadcasted_iota(jnp.int32, last.shape, 1)
        mark = jnp.where(column == me, (limit + MARK).astype(jnp.float32), 0.0)
        unfilled = jnp.where(limit < BLOCK, CHUNK - 1, CHUNK)
        ref[BLOCK - CHUNK:, :] = jnp.where(row == unfilled, mark, last).astype(ref.dtype)


def arrange(tokens, heads, rank_ref, own_ref, other_ref, weight_ref, q_ref, w_ref):
    half = tokens // 2

    def step(token, _):
        for ref, first in ((own_ref, 0), (other_ref, half)):
            to = pl.multiple_of(rank_ref[first + token] * heads, heads)
            start = pl.multiple_of(token * heads, heads)
            q_ref[pl.ds(to, heads), :] = ref[pl.ds(start, heads), :]
            w_ref[pl.ds(to, heads), :] = weight_ref[pl.ds(pl.multiple_of((first + token) * heads, heads), heads), :]
        return 0

    lax.fori_loop(0, half, step, 0, unroll=2)


def lane_of(chunk):
    return (chunk & 7) * 16 + ((chunk >> 3) & 1) * 8 + ((chunk >> 4) & 1) * 4 + ((chunk >> 5) & 1) * 2 + ((chunk >> 6) & 1)


def folded(a, b, step, lane):
    return jnp.where(
        (lane & step) == 0,
        jnp.maximum(a, pltpu.roll(a, 128 - step, 1)),
        jnp.maximum(b, pltpu.roll(b, step, 1)),
    )


def scores(tokens, heads, stride, sorted_ref, place_ref, q_ref, w_ref, at_ref, row0_ref, row1_ref, row2_ref, row3_ref,
           pooled_ref, slab_ref, packed_ref, seen_ref, score_ref, max_ref, limit_ref, limit_smem, first_smem, sem, *accs):
    blocks = slab_ref.shape[0] // BLOCK
    piece = 2 * BLOCK
    per_row = SIDES * 2
    most = max_ref.shape[0]
    rows = GROUP // 2 * heads
    plane = place_ref[2]
    lane1 = lax.broadcasted_iota(jnp.int32, (1, 128), 1)
    lane = lax.broadcasted_iota(jnp.int32, (8, 128), 1)
    wide = lax.broadcasted_iota(jnp.int32, (tokens, 128), 1)

    for y_step, row_ref in zip(STEPS, (row0_ref, row1_ref, row2_ref, row3_ref)):
        y = (place_ref[0] + SIDES - y_step) % SIDES
        for spot, x_step in enumerate(STEPS):
            x = (place_ref[1] + SIDES - x_step) % SIDES
            to = pl.multiple_of((y * SIDES + x) * piece, piece)
            slab_ref[pl.ds(to, piece), :] = row_ref[spot * piece:(spot + 1) * piece, :]

    def shard_of(block):
        return (block // per_row) * (2 * per_row) + plane * per_row + block % per_row

    marks = slab_ref[pl.ds(BLOCK - CHUNK, CHUNK), :]
    for block in range(1, blocks):
        marks = jnp.maximum(marks, slab_ref[pl.ds(block * BLOCK + BLOCK - CHUNK, CHUNK), :])
    mark = marks.astype(jnp.float32)[CHUNK - 1:CHUNK, :]
    limit = jnp.where(mark > MARK / 2, mark - MARK, float(BLOCK)).astype(jnp.int32)
    limit_ref[...] = jnp.broadcast_to(limit, limit_ref.shape)
    copy = pltpu.make_async_copy(limit_ref, limit_smem, sem)
    copy.start()
    max_ref[...] = jnp.full(max_ref.shape, mask_value, jnp.float32)
    copy.wait()

    inside = lane % CHUNK

    def pack(block, at):
        shard = shard_of(block)
        filled = limit_smem[0, shard]
        first = place_ref[3] + shard * stride
        for part in range(PARTS):
            packed_ref[pl.ds(pl.multiple_of((at + part) * CHUNK, CHUNK), CHUNK), :] = slab_ref[
                pl.ds(pl.multiple_of(block * BLOCK + part * CHUNK, CHUNK), CHUNK), :
            ]
            offset = inside + part * CHUNK
            seen_ref[at + part] = jnp.where(offset < filled, offset + first, FAR)
            first_smem[at + part] = first + part * CHUNK
        return at + (filled + (CHUNK - 1)) // CHUNK

    total = lax.fori_loop(0, blocks, pack, jnp.int32(0), unroll=4)
    for slot in range(SLOTS):
        seen_ref[total + slot] = jnp.full((8, 128), FAR, jnp.int32)

    def count(tile):
        first = first_smem[tile * SLOTS]
        groups = jnp.int32(0)
        for group in range(tokens // GROUP):
            groups = groups + (sorted_ref[group * GROUP] >= first).astype(jnp.int32)
        return groups

    tiles = (total + SLOTS - 1) // SLOTS
    active = jnp.int32(0)
    for tile in range(most):
        active = active + ((tile < tiles) & (sorted_ref[0] >= first_smem[tile * SLOTS])).astype(jnp.int32)

    def push(tile):
        keys = packed_ref[pl.ds(pl.multiple_of(tile * TILE, TILE), TILE), :]
        keys = jnp.concatenate([keys, jnp.zeros_like(keys)], axis=1)
        for side in range(2):
            pltpu.matmul_push_rhs(keys, 0, side, transpose=True)

    def issue(group, pair, load=None):
        for side, acc in enumerate(pair):
            start = pl.multiple_of(group * (2 * rows) + side * rows, rows)
            left = q_ref[pl.ds(start, rows), :]
            pltpu.matmul_acc_lhs(acc, jnp.concatenate([left, left], axis=1), load)

    def finish(tile, group, pair):
        halves = []
        for side, acc in enumerate(pair):
            weights = w_ref[pl.ds(pl.multiple_of(group * (2 * rows) + side * rows, rows), rows), :]
            raw = pltpu.matmul_pop(acc)
            halves.append(
                [
                    (jnp.maximum(raw[:, part * 128:part * 128 + 128], 0.0) * weights).reshape(-1, heads // 8, 8, 128).sum(1)
                    for part in range(2)
                ]
            )
        for part in range(2):
            both = jnp.concatenate([halves[0][part], halves[1][part]], axis=0)
            score_ref[2 * tile + part, pl.ds(pl.multiple_of(group * GROUP, GROUP), GROUP), :] = both.sum(1)

    @pl.when(active > 0)
    def _():
        push(0)
        issue(0, accs[:2], 0)

        def tile_step(tile, _):
            groups = count(tile)
            odd = groups % 2
            push(jnp.minimum(tile + 1, active - 1))

            def pair_step(pair, _):
                issue(2 * pair + 1, accs[2:])
                finish(tile, 2 * pair, accs[:2])
                issue(2 * pair + 2, accs[:2])
                finish(tile, 2 * pair + 1, accs[2:])
                return 0

            lax.fori_loop(0, groups // 2 - 1 + odd, pair_step, 0)

            @pl.when(odd == 1)
            def _():
                finish(tile, groups - 1, accs[:2])
                issue(0, accs[:2], 0)

            @pl.when(odd == 0)
            def _():
                issue(groups - 1, accs[2:])
                finish(tile, groups - 2, accs[:2])
                issue(0, accs[:2], 0)
                finish(tile, groups - 1, accs[2:])

            return 0

        lax.fori_loop(0, active, tile_step, 0)
        for acc in accs[:2]:
            pltpu.matmul_pop(acc)

    def reduce_step(tile, _):
        seen = []
        for part in range(2):
            slot = tile * SLOTS + part * 8
            value = seen_ref[slot]
            for chunk in range(1, 8):
                value = jnp.where(lane // CHUNK == chunk, seen_ref[slot + chunk], value)
            seen.append(value[:1])
        found = [jnp.where(seen[part] <= at_ref[...], score_ref[2 * tile + part], mask_value) for part in range(2)]
        max_ref[tile] = folded(found[0], found[1], 8, wide)
        return 0

    lax.fori_loop(0, active, reduce_step, 0)
    found = [max_ref[tile] for tile in range(most)]
    for step in (4, 2, 1):
        found = [folded(a, b, step, wide) for a, b in zip(found[::2], found[1::2])]
    chunks = jnp.where((lane1 < 2 * blocks) & ((lane1 // per_row) % 2 == plane), (limit + (CHUNK - 1)) // CHUNK, 0)
    upto = chunks
    step = 1
    while step < 2 * blocks:
        upto = upto + jnp.where(lane1 >= step, pltpu.roll(upto, step, 1), 0)
        step *= 2
    before = upto - chunks
    pooled = None
    for part in range(PARTS):
        chunk = before + jnp.minimum(part, jnp.maximum(chunks - 1, 0))
        chunk = jnp.broadcast_to(jnp.minimum(chunk, most * SLOTS - 1), (tokens, 128))
        spot = lane_of(chunk)
        value = jnp.take_along_axis(found[0], spot, axis=1)
        if len(found) > 1:
            value = jnp.where(chunk < 128, value, jnp.take_along_axis(found[1], spot, axis=1))
        pooled = value if pooled is None else jnp.maximum(pooled, value)
    pooled_ref[...] = pooled.astype(jnp.bfloat16)


def restore(plane_ref, unsort_ref, spread_ref, near_ref, far_ref, mine_ref, theirs_ref):
    half = mine_ref.shape[0]
    lane = lax.broadcasted_iota(jnp.int32, near_ref.shape, 1)
    near = (lane // (2 * SIDES)) % 2 == plane_ref[0]
    pooled = jnp.where(near, near_ref[...].astype(jnp.float32), far_ref[...].astype(jnp.float32)).astype(jnp.bfloat16)
    ordered = jnp.dot(unsort_ref[...], pooled, preferred_element_type=jnp.float32).astype(jnp.bfloat16)
    placed = jnp.dot(ordered, spread_ref[...], preferred_element_type=jnp.float32).astype(jnp.bfloat16)
    mine_ref[...] = placed[:half]
    theirs_ref[...] = placed[half:]


def body(queries, head_weights, keys, query_pos, block_limits):
    shards = lax.axis_size("blk")
    me = lax.axis_index("blk")
    core = me % 2
    member = lax.axis_index("team")
    quarter = 2 * member + core
    count, heads, head_size = queries.shape
    tokens = 2 * count
    local_blocks = keys.shape[0] // BLOCK
    cores = [(i, i ^ 1) for i in range(shards)]
    smem = pl.BlockSpec(memory_space=pltpu.SMEM)
    vmem = pl.BlockSpec(memory_space=pltpu.VMEM)

    own = queries.reshape(count * heads, head_size)
    other = swapped(own, cores, "blk")
    other_pos = swapped(query_pos, cores, "blk")
    other_weights = swapped(head_weights, cores, "blk")

    piece_shape = jax.ShapeDtypeStruct((BLOCK, head_size), keys.dtype)
    keep, give = pl.pallas_call(
        marked,
        out_shape=(piece_shape, piece_shape),
        in_specs=[pl.BlockSpec(memory_space=pl.ANY)] * 2,
        out_specs=(vmem, vmem),
        scratch_shapes=[pltpu.SMEM(block_limits.shape, jnp.int32), pltpu.SemaphoreType.DMA((3,))],
        compiler_params=pltpu.CompilerParams(vmem_limit_bytes=4 * 2**20),
        name="marked",
    )(block_limits, keys)
    got = swapped(give, cores, "blk")
    piece = jnp.where(core == 0, jnp.stack([keep, got]), jnp.stack([got, keep]))

    def moved(y_step, z_step, x_step):
        pairs = []
        for source in range(shards):
            c, x, z, y = source % 2, source // 2 % SIDES, source // (2 * SIDES) % 2, source // (4 * SIDES)
            x, z, y = (x + x_step) % SIDES, (z + z_step) % 2, (y + y_step) % SIDES
            pairs.append((source, ((y * 2 + z) * SIDES + x) * 2 + c))
        return pairs

    piece = piece.reshape(2 * BLOCK, head_size)
    pieces = [piece] + [swapped(piece, moved(0, 0, step), "blk") for step in STEPS[1:]]

    piece, other_pos, other_weights = lax.optimization_barrier((piece, other_pos, other_weights))
    positions = jnp.concatenate([query_pos, other_pos])
    weights = jnp.concatenate([head_weights, other_weights]) * head_size ** (-0.5)
    wide = jnp.broadcast_to(weights.reshape(tokens * heads, 1), (tokens * heads, 128))

    index = jnp.arange(tokens, dtype=jnp.int32)
    ahead = (positions[None, :] > positions[:, None]) | (
        (positions[None, :] == positions[:, None]) & (index[None, :] < index[:, None])
    )
    rank = jnp.sum(ahead.astype(jnp.int32), axis=1)
    hit = rank[None, :] == index[:, None]
    in_order = jnp.sum(jnp.where(hit, positions[None, :], 0), axis=1)
    at = jnp.broadcast_to(in_order[:, None], (tokens, 128))
    unsort = (rank[:, None] == index[None, :]).astype(jnp.bfloat16)
    lane = jnp.arange(128, dtype=jnp.int32)
    target = lane * local_blocks + quarter
    spread = ((lane < shards)[:, None] & (target[:, None] == jnp.arange(shards * local_blocks)[None, :])).astype(jnp.bfloat16)

    q_rows, w_rows = pl.pallas_call(
        lambda *refs: arrange(tokens, heads, *refs),
        out_shape=(
            jax.ShapeDtypeStruct((tokens * heads, head_size), jnp.bfloat16),
            jax.ShapeDtypeStruct((tokens * heads, 128), jnp.float32),
        ),
        in_specs=[smem] + [vmem] * 3,
        out_specs=(vmem, vmem),
        compiler_params=pltpu.CompilerParams(vmem_limit_bytes=4 * 2**20),
        cost_estimate=pl.CostEstimate(flops=0, bytes_accessed=12 * 2**20, transcendentals=0),
        name="arranged",
    )(rank, own, other, wide)

    q_rows, w_rows, pieces = lax.optimization_barrier((q_rows, w_rows, pieces))
    row = jnp.concatenate(pieces)
    near = [row] + [swapped(row, moved(step, 0, 0), "blk") for step in STEPS[1:]]
    far = [swapped(value, moved(0, 1, 0), "blk") for value in near]

    result = jax.ShapeDtypeStruct((count, shards * local_blocks), jnp.bfloat16)
    slots = shards // 2 * PARTS
    accs = [pltpu.ACC(side)((GROUP // 2 * heads, TILE), jnp.float32) for _ in range(2) for side in range(2)]

    def kernel(*refs):
        pl.run_scoped(lambda *accs: scores(tokens, heads, local_blocks * BLOCK, *refs, *accs), *accs)

    def pooled(values, plane):
        place = jnp.stack([me // (4 * SIDES), me // 2 % SIDES, plane, quarter * BLOCK]).astype(jnp.int32)
        return pl.pallas_call(
            kernel,
            out_shape=jax.ShapeDtypeStruct((tokens, 128), jnp.bfloat16),
            in_specs=[smem] * 2 + [vmem] * 7,
            out_specs=vmem,
            scratch_shapes=[
                pltpu.VMEM((shards // 2 * BLOCK, head_size), jnp.bfloat16),
                pltpu.VMEM(((slots + PARTS) * CHUNK, head_size), jnp.bfloat16),
                pltpu.VMEM((slots + SLOTS, 8, 128), jnp.int32),
                pltpu.VMEM((2 * (slots // SLOTS), tokens, 128), jnp.float32),
                pltpu.VMEM((slots // SLOTS, tokens, 128), jnp.float32),
                pltpu.VMEM((8, 128), jnp.int32),
                pltpu.SMEM((8, 128), jnp.int32),
                pltpu.SMEM((slots + PARTS,), jnp.int32),
                pltpu.SemaphoreType.DMA(()),
            ],
            compiler_params=pltpu.CompilerParams(vmem_limit_bytes=8 * 2**20),
            cost_estimate=pl.CostEstimate(flops=2**32, bytes_accessed=8 * 2**20, transcendentals=0),
            name="pooled_scores",
        )(in_order, place, q_rows, w_rows, at, *values)

    plane = me // (2 * SIDES) % 2
    mine, theirs = pl.pallas_call(
        restore,
        out_shape=(result, result),
        in_specs=[smem] + [vmem] * 4,
        out_specs=(vmem, vmem),
        compiler_params=pltpu.CompilerParams(vmem_limit_bytes=4 * 2**20),
        name="restored",
    )(plane[None].astype(jnp.int32), unsort, spread, pooled(near, plane), pooled(far, 1 - plane))
    chip = mine + swapped(theirs, cores, "blk")
    return (chip + swapped(chip, [(0, 1), (1, 0)], "team")).astype(jnp.float32)


def solution(mesh):
    in_specs = (P("blk", None, None), P("blk", None), P("blk", None), P("blk"), P("blk"))
    out_specs = P("blk", None)

    def step(*args):
        with jax.sharding.use_abstract_mesh(mesh.abstract_mesh):
            return jax.shard_map(body, mesh=mesh, in_specs=in_specs, out_specs=out_specs, check_vma=False)(*args)

    return step
```

```python
import jax
import jax.numpy as jnp
from jax import lax
from jax.experimental import pallas as pl
from jax.experimental.pallas import tpu as pltpu
from jax.sharding import PartitionSpec as P

BLOCK = 64
CHUNK = 16
GROUP = 16
TILE = 256
PARTS = BLOCK // CHUNK
SLOTS = TILE // CHUNK
MARK = 100.0
SIDES = 4
STEPS = (0, 1, 3, 2)
FAR = 1 << 30
mask_value = -8.0


def swapped(value, pairs, axis):
    return lax.ppermute(value, axis, pairs)


def marked(limit_hbm, key_hbm, keep_ref, give_ref, limit_ref, sems):
    me = lax.axis_index("blk")
    keep = 2 * lax.axis_index("team") + me % 2
    picks = ((keep_ref, keep), (give_ref, keep + 1 - 2 * (keep % 2)))
    copies = [pltpu.make_async_copy(limit_hbm, limit_ref, sems.at[2])]
    for n, (ref, block) in enumerate(picks):
        start = pl.multiple_of(block * BLOCK, BLOCK)
        copies.append(pltpu.make_async_copy(key_hbm.at[pl.ds(start, BLOCK), :], ref, sems.at[n]))
    for copy in copies:
        copy.start()
    for copy in copies:
        copy.wait()
    for ref, block in picks:
        limit = limit_ref[block]
        last = ref[BLOCK - CHUNK:, :].astype(jnp.float32)
        row = lax.broadcasted_iota(jnp.int32, last.shape, 0)
        column = lax.broadcasted_iota(jnp.int32, last.shape, 1)
        mark = jnp.where(column == me, (limit + MARK).astype(jnp.float32), 0.0)
        unfilled = jnp.where(limit < BLOCK, CHUNK - 1, CHUNK)
        ref[BLOCK - CHUNK:, :] = jnp.where(row == unfilled, mark, last).astype(ref.dtype)


def arrange(tokens, heads, scale, rank_ref, own_ref, other_ref, own_weight_ref, other_weight_ref, q_ref, w_ref):
    half = tokens // 2

    def step(token, _):
        start = pl.multiple_of(token * heads, heads)
        for ref, weight_ref, first in ((own_ref, own_weight_ref, 0), (other_ref, other_weight_ref, half)):
            to = pl.multiple_of(rank_ref[first + token] * heads, heads)
            q_ref[pl.ds(to, heads), :] = ref[pl.ds(start, heads), :]
            w_ref[pl.ds(to, heads), :] = weight_ref[pl.ds(start, heads), :] * scale
        return 0

    lax.fori_loop(0, half, step, 0, unroll=4)


def lane_of(chunk):
    return (chunk & 7) * 16 + ((chunk >> 3) & 1) * 8 + ((chunk >> 4) & 1) * 4 + ((chunk >> 5) & 1) * 2 + ((chunk >> 6) & 1)


def folded(a, b, step, lane):
    return jnp.where(
        (lane & step) == 0,
        jnp.maximum(a, pltpu.roll(a, 128 - step, 1)),
        jnp.maximum(b, pltpu.roll(b, step, 1)),
    )


def scores(tokens, heads, stride, sorted_ref, place_ref, q_ref, w_ref, at_ref, row_ref, rest_ref,
           pooled_ref, slab_ref, packed_ref, score_ref, max_ref, first_smem, *accs):
    blocks = slab_ref.shape[0] // BLOCK
    piece = 2 * BLOCK
    per_row = SIDES * 2
    most = max_ref.shape[0]
    rows = GROUP // 2 * heads
    plane = place_ref[2]
    lane1 = lax.broadcasted_iota(jnp.int32, (1, 128), 1)
    lane = lax.broadcasted_iota(jnp.int32, (8, 128), 1)
    wide = lax.broadcasted_iota(jnp.int32, (tokens, 128), 1)

    marks = None
    for ref in (row_ref, rest_ref):
        for end in range(BLOCK, ref.shape[0] + 1, BLOCK):
            last = ref[end - CHUNK:end, :]
            marks = last if marks is None else jnp.maximum(marks, last)
    mark = marks.astype(jnp.float32)[CHUNK - 1:CHUNK, :]
    limit = jnp.where(mark > MARK / 2, mark - MARK, float(BLOCK)).astype(jnp.int32)
    chunks = jnp.where((lane1 < 2 * blocks) & ((lane1 // per_row) % 2 == plane), (limit + (CHUNK - 1)) // CHUNK, 0)
    upto = chunks
    step = 1
    while step < 2 * blocks:
        upto = upto + jnp.where(lane1 >= step, pltpu.roll(upto, step, 1), 0)
        step *= 2
    before = upto - chunks
    square = (128, 128)
    down = jnp.broadcast_to(upto.astype(jnp.float32), square).T
    at_chunk = lax.broadcasted_iota(jnp.int32, square, 1).astype(jnp.float32)
    earlier = (down <= at_chunk) & (lax.broadcasted_iota(jnp.int32, square, 0) < 2 * blocks)
    shard = jnp.sum(earlier.astype(jnp.float32), axis=0, keepdims=True).astype(jnp.int32)
    shard = jnp.broadcast_to(jnp.minimum(shard, 2 * blocks - 1), (8, 128))
    skipped = (lane - jnp.take_along_axis(jnp.broadcast_to(before, (8, 128)), shard, axis=1)) * CHUNK
    position = place_ref[3] + shard * stride + skipped
    held = jnp.take_along_axis(jnp.broadcast_to(limit, (8, 128)), shard, axis=1) - skipped
    total = jnp.max(upto, axis=1, keepdims=True)
    held = jnp.where(lane < total, held, 0)
    length = SIDES * piece
    for y_step, ref, start in zip(STEPS, (row_ref, rest_ref, rest_ref, rest_ref), (0, 0, length, 2 * length)):
        y = (place_ref[0] + SIDES - y_step) % SIDES
        for spot, x_step in enumerate(STEPS):
            x = (place_ref[1] + SIDES - x_step) % SIDES
            to = pl.multiple_of((y * SIDES + x) * piece, piece)
            slab_ref[pl.ds(to, piece), :] = ref[start + spot * piece:start + (spot + 1) * piece, :]

    max_ref[...] = jnp.full(max_ref.shape, mask_value, jnp.float32)
    before_here = pltpu.roll(before, (128 - plane * per_row) % 128, 1)
    for block in range(blocks):
        at = before_here[0, (block // per_row) * (2 * per_row) + block % per_row]
        for part in range(PARTS):
            start = block * BLOCK + part * CHUNK
            packed_ref[pl.ds(pl.multiple_of((at + part) * CHUNK, CHUNK), CHUNK), :] = slab_ref[start:start + CHUNK, :]
    total = upto[0, 2 * blocks - 1]
    firsts = [position[0, tile * SLOTS] for tile in range(most)]
    for tile in range(most):
        first_smem[tile] = firsts[tile]

    def count(tile):
        first = first_smem[tile]
        groups = jnp.int32(0)
        for group in range(tokens // GROUP):
            groups = groups + (sorted_ref[group * GROUP] >= first).astype(jnp.int32)
        return groups

    tiles = (total + SLOTS - 1) // SLOTS
    active = jnp.int32(0)
    for tile in range(most):
        active = active + ((tile < tiles) & (sorted_ref[0] >= firsts[tile])).astype(jnp.int32)

    def push(tile):
        keys = packed_ref[pl.ds(pl.multiple_of(tile * TILE, TILE), TILE), :]
        keys = jnp.concatenate([keys, jnp.zeros_like(keys)], axis=1)
        for side in range(2):
            pltpu.matmul_push_rhs(keys, 0, side, transpose=True)

    def issue(group, pair, load=None):
        for side, acc in enumerate(pair):
            start = pl.multiple_of(group * (2 * rows) + side * rows, rows)
            left = q_ref[pl.ds(start, rows), :]
            pltpu.matmul_acc_lhs(acc, jnp.concatenate([left, left], axis=1), load)

    def finish(tile, group, pair):
        halves = []
        for side, acc in enumerate(pair):
            weights = w_ref[pl.ds(pl.multiple_of(group * (2 * rows) + side * rows, rows), rows), :]
            raw = pltpu.matmul_pop(acc)
            halves.append(
                [
                    (jnp.maximum(raw[:, part * 128:part * 128 + 128], 0.0) * weights).reshape(-1, heads // 8, 8, 128).sum(1)
                    for part in range(2)
                ]
            )
        for part in range(2):
            both = jnp.concatenate([halves[0][part], halves[1][part]], axis=0)
            score_ref[2 * tile + part, pl.ds(pl.multiple_of(group * GROUP, GROUP), GROUP), :] = both.sum(1)

    @pl.when(active > 0)
    def _():
        push(0)
        issue(0, accs[:2], 0)

        def tile_step(tile, _):
            groups = count(tile)
            odd = groups % 2
            later = jnp.minimum(tile + 1, active - 1)

            def pair_step(pair, _):
                issue(2 * pair + 1, accs[2:])
                finish(tile, 2 * pair, accs[:2])
                issue(2 * pair + 2, accs[:2])
                finish(tile, 2 * pair + 1, accs[2:])
                return 0

            lax.fori_loop(0, groups // 2 - 1 + odd, pair_step, 0)

            @pl.when(odd == 1)
            def _():
                push(later)
                finish(tile, groups - 1, accs[:2])
                issue(0, accs[:2], 0)

            @pl.when(odd == 0)
            def _():
                issue(groups - 1, accs[2:])
                push(later)
                finish(tile, groups - 2, accs[:2])
                issue(0, accs[:2], 0)
                finish(tile, groups - 1, accs[2:])

            return 0

        lax.fori_loop(0, active, tile_step, 0)
        for acc in accs[:2]:
            pltpu.matmul_pop(acc)

    def reduce_step(tile, _):
        seen = []
        for part in range(2):
            chunk = tile * SLOTS + part * 8 + lane // CHUNK
            filled = lane % CHUNK < jnp.take_along_axis(held, chunk, axis=1)
            value = jnp.take_along_axis(position, chunk, axis=1) + lane % CHUNK
            seen.append(jnp.where(filled, value, FAR)[:1])
        found = [jnp.where(seen[part] <= at_ref[...], score_ref[2 * tile + part], mask_value) for part in range(2)]
        max_ref[tile] = folded(found[0], found[1], 8, wide)
        return 0

    lax.fori_loop(0, active, reduce_step, 0)
    found = [max_ref[tile] for tile in range(most)]
    for step in (4, 2, 1):
        found = [folded(a, b, step, wide) for a, b in zip(found[::2], found[1::2])]
    pooled = None
    for part in range(PARTS):
        chunk = before + jnp.minimum(part, jnp.maximum(chunks - 1, 0))
        chunk = jnp.broadcast_to(jnp.minimum(chunk, most * SLOTS - 1), (tokens, 128))
        spot = lane_of(chunk)
        value = jnp.take_along_axis(found[0], spot, axis=1)
        if len(found) > 1:
            value = jnp.where(chunk < 128, value, jnp.take_along_axis(found[1], spot, axis=1))
        pooled = value if pooled is None else jnp.maximum(pooled, value)
    pooled_ref[...] = pooled.astype(jnp.bfloat16)


def restore(plane_ref, unsort_ref, spread_ref, near_ref, far_ref, mine_ref, theirs_ref):
    half = mine_ref.shape[0]
    lane = lax.broadcasted_iota(jnp.int32, near_ref.shape, 1)
    near = (lane // (2 * SIDES)) % 2 == plane_ref[0]
    pooled = jnp.where(near, near_ref[...].astype(jnp.float32), far_ref[...].astype(jnp.float32)).astype(jnp.bfloat16)
    ordered = jnp.dot(unsort_ref[...], pooled, preferred_element_type=jnp.float32).astype(jnp.bfloat16)
    placed = jnp.dot(ordered, spread_ref[...], preferred_element_type=jnp.float32).astype(jnp.bfloat16)
    mine_ref[...] = placed[:half]
    theirs_ref[...] = placed[half:]


def body(queries, head_weights, keys, query_pos, block_limits):
    shards = lax.axis_size("blk")
    me = lax.axis_index("blk")
    core = me % 2
    member = lax.axis_index("team")
    quarter = 2 * member + core
    count, heads, head_size = queries.shape
    tokens = 2 * count
    local_blocks = keys.shape[0] // BLOCK
    cores = [(i, i ^ 1) for i in range(shards)]
    smem = pl.BlockSpec(memory_space=pltpu.SMEM)
    vmem = pl.BlockSpec(memory_space=pltpu.VMEM)

    own = queries.reshape(count * heads, head_size)
    other = swapped(own, cores, "blk")
    other_pos = swapped(query_pos, cores, "blk")
    other_weights = swapped(head_weights, cores, "blk")

    piece_shape = jax.ShapeDtypeStruct((BLOCK, head_size), keys.dtype)
    keep, give = pl.pallas_call(
        marked,
        out_shape=(piece_shape, piece_shape),
        in_specs=[pl.BlockSpec(memory_space=pl.ANY)] * 2,
        out_specs=(vmem, vmem),
        scratch_shapes=[pltpu.SMEM(block_limits.shape, jnp.int32), pltpu.SemaphoreType.DMA((3,))],
        compiler_params=pltpu.CompilerParams(vmem_limit_bytes=4 * 2**20),
        name="marked",
    )(block_limits, keys)
    got = swapped(give, cores, "blk")
    piece = jnp.where(core == 0, jnp.stack([keep, got]), jnp.stack([got, keep]))

    def moved(y_step, z_step, x_step):
        pairs = []
        for source in range(shards):
            c, x, z, y = source % 2, source // 2 % SIDES, source // (2 * SIDES) % 2, source // (4 * SIDES)
            x, z, y = (x + x_step) % SIDES, (z + z_step) % 2, (y + y_step) % SIDES
            pairs.append((source, ((y * 2 + z) * SIDES + x) * 2 + c))
        return pairs

    piece = piece.reshape(2 * BLOCK, head_size)
    pieces = [piece] + [swapped(piece, moved(0, 0, step), "blk") for step in STEPS[1:]]

    row = jnp.concatenate(pieces)
    row, query_pos, head_weights, other_pos, other_weights = lax.optimization_barrier(
        (row, query_pos, head_weights, other_pos, other_weights)
    )
    positions = jnp.concatenate([query_pos, other_pos])
    wide = [
        jnp.broadcast_to(value.reshape(count * heads, 1), (count * heads, 128)) for value in (head_weights, other_weights)
    ]

    index = jnp.arange(tokens, dtype=jnp.int32)
    ahead = (positions[None, :] > positions[:, None]) | (
        (positions[None, :] == positions[:, None]) & (index[None, :] < index[:, None])
    )
    rank = jnp.sum(ahead.astype(jnp.int32), axis=1)
    hit = rank[None, :] == index[:, None]
    in_order = jnp.sum(jnp.where(hit, positions[None, :], 0), axis=1)
    at = jnp.broadcast_to(in_order[:, None], (tokens, 128))
    unsort = (rank[:, None] == index[None, :]).astype(jnp.bfloat16)
    lane = jnp.arange(128, dtype=jnp.int32)
    target = lane * local_blocks + quarter
    spread = ((lane < shards)[:, None] & (target[:, None] == jnp.arange(shards * local_blocks)[None, :])).astype(jnp.bfloat16)

    q_rows, w_rows = pl.pallas_call(
        lambda *refs: arrange(tokens, heads, head_size ** (-0.5), *refs),
        out_shape=(
            jax.ShapeDtypeStruct((tokens * heads, head_size), jnp.bfloat16),
            jax.ShapeDtypeStruct((tokens * heads, 128), jnp.float32),
        ),
        in_specs=[smem] + [vmem] * 4,
        out_specs=(vmem, vmem),
        compiler_params=pltpu.CompilerParams(vmem_limit_bytes=4 * 2**20),
        cost_estimate=pl.CostEstimate(flops=0, bytes_accessed=12 * 2**20, transcendentals=0),
        name="arranged",
    )(rank, own, other, *wide)

    rest = [swapped(row, moved(step, 0, 0), "blk") for step in STEPS[1:]]
    rest, q_rows, w_rows = lax.optimization_barrier((rest, q_rows, w_rows))
    rest = jnp.concatenate(rest)
    near = [row, rest]
    far = [swapped(value, moved(0, 1, 0), "blk") for value in near]

    result = jax.ShapeDtypeStruct((count, shards * local_blocks), jnp.bfloat16)
    slots = shards // 2 * PARTS
    accs = [pltpu.ACC(side)((GROUP // 2 * heads, TILE), jnp.float32) for _ in range(2) for side in range(2)]

    def kernel(*refs):
        pl.run_scoped(lambda *accs: scores(tokens, heads, local_blocks * BLOCK, *refs, *accs), *accs)

    def pooled(values, plane):
        place = jnp.stack([me // (4 * SIDES), me // 2 % SIDES, plane, quarter * BLOCK]).astype(jnp.int32)
        return pl.pallas_call(
            kernel,
            out_shape=jax.ShapeDtypeStruct((tokens, 128), jnp.bfloat16),
            in_specs=[smem] * 2 + [vmem] * 5,
            out_specs=vmem,
            scratch_shapes=[
                pltpu.VMEM((shards // 2 * BLOCK, head_size), jnp.bfloat16),
                pltpu.VMEM(((slots + PARTS) * CHUNK, head_size), jnp.bfloat16),
                    pltpu.VMEM((2 * (slots // SLOTS), tokens, 128), jnp.float32),
                pltpu.VMEM((slots // SLOTS, tokens, 128), jnp.float32),
                pltpu.SMEM((slots // SLOTS,), jnp.int32),
            ],
            compiler_params=pltpu.CompilerParams(vmem_limit_bytes=8 * 2**20),
            cost_estimate=pl.CostEstimate(flops=2**32, bytes_accessed=8 * 2**20, transcendentals=0),
            name="pooled_scores",
        )(in_order, place, q_rows, w_rows, at, *values)

    plane = me // (2 * SIDES) % 2
    mine, theirs = pl.pallas_call(
        restore,
        out_shape=(result, result),
        in_specs=[smem] + [vmem] * 4,
        out_specs=(vmem, vmem),
        compiler_params=pltpu.CompilerParams(vmem_limit_bytes=4 * 2**20),
        name="restored",
    )(plane[None].astype(jnp.int32), unsort, spread, pooled(near, plane), pooled(far, 1 - plane))
    chip = mine + swapped(theirs, cores, "blk")
    return (chip + swapped(chip, [(0, 1), (1, 0)], "team")).astype(jnp.float32)


def solution(mesh):
    in_specs = (P("blk", None, None), P("blk", None), P("blk", None), P("blk"), P("blk"))
    out_specs = P("blk", None)

    def step(*args):
        with jax.sharding.use_abstract_mesh(mesh.abstract_mesh):
            return jax.shard_map(body, mesh=mesh, in_specs=in_specs, out_specs=out_specs, check_vma=False)(*args)

    return step
```

```python
import jax
import jax.numpy as jnp
from jax import lax
from jax.experimental import pallas as pl
from jax.experimental.pallas import tpu as pltpu
from jax.sharding import PartitionSpec as P

BLOCK = 64
CHUNK = 16
GROUP = 16
TILE = 256
PARTS = BLOCK // CHUNK
SLOTS = TILE // CHUNK
MARK = 100.0
SIDES = 4
STEPS = (0, 1, 3, 2)
FAR = 1 << 30
mask_value = -8.0


def swapped(value, pairs, axis):
    return lax.ppermute(value, axis, pairs)


def marked(limit_hbm, key_hbm, keep_ref, give_ref, limit_ref, sems):
    me = lax.axis_index("blk")
    keep = 2 * lax.axis_index("team") + me % 2
    picks = ((keep_ref, keep), (give_ref, keep + 1 - 2 * (keep % 2)))
    copies = [pltpu.make_async_copy(limit_hbm, limit_ref, sems.at[2])]
    for n, (ref, block) in enumerate(picks):
        start = pl.multiple_of(block * BLOCK, BLOCK)
        copies.append(pltpu.make_async_copy(key_hbm.at[pl.ds(start, BLOCK), :], ref, sems.at[n]))
    for copy in copies:
        copy.start()
    for copy in copies:
        copy.wait()
    for ref, block in picks:
        limit = limit_ref[block]
        last = ref[BLOCK - CHUNK:, :].astype(jnp.float32)
        row = lax.broadcasted_iota(jnp.int32, last.shape, 0)
        column = lax.broadcasted_iota(jnp.int32, last.shape, 1)
        mark = jnp.where(column == me, (limit + MARK).astype(jnp.float32), 0.0)
        unfilled = jnp.where(limit < BLOCK, CHUNK - 1, CHUNK)
        ref[BLOCK - CHUNK:, :] = jnp.where(row == unfilled, mark, last).astype(ref.dtype)


def arrange(tokens, heads, scale, rank_ref, own_ref, other_ref, own_weight_ref, other_weight_ref, q_ref, w_ref):
    half = tokens // 2

    def step(token, _):
        start = pl.multiple_of(token * heads, heads)
        for ref, weight_ref, first in ((own_ref, own_weight_ref, 0), (other_ref, other_weight_ref, half)):
            to = pl.multiple_of(rank_ref[first + token] * heads, heads)
            q_ref[pl.ds(to, heads), :] = ref[pl.ds(start, heads), :]
            w_ref[pl.ds(to, heads), :] = weight_ref[pl.ds(start, heads), :] * scale
        return 0

    lax.fori_loop(0, half, step, 0, unroll=4)


def lane_of(chunk):
    return (chunk & 7) * 16 + ((chunk >> 3) & 1) * 8 + ((chunk >> 4) & 1) * 4 + ((chunk >> 5) & 1) * 2 + ((chunk >> 6) & 1)


def folded(a, b, step, lane):
    return jnp.where(
        (lane & step) == 0,
        jnp.maximum(a, pltpu.roll(a, 128 - step, 1)),
        jnp.maximum(b, pltpu.roll(b, step, 1)),
    )


def scores(tokens, heads, stride, sorted_ref, place_ref, q_ref, w_ref, at_ref, row_ref, rest_ref,
           pooled_ref, slab_ref, packed_ref, score_ref, max_ref, first_smem, *accs):
    blocks = slab_ref.shape[0] // BLOCK
    piece = 2 * BLOCK
    per_row = SIDES * 2
    most = max_ref.shape[0]
    rows = GROUP // 2 * heads
    plane = place_ref[2]
    lane1 = lax.broadcasted_iota(jnp.int32, (1, 128), 1)
    lane = lax.broadcasted_iota(jnp.int32, (8, 128), 1)
    wide = lax.broadcasted_iota(jnp.int32, (tokens, 128), 1)

    marks = None
    for ref in (row_ref, rest_ref):
        for end in range(BLOCK, ref.shape[0] + 1, BLOCK):
            last = ref[end - CHUNK:end, :]
            marks = last if marks is None else jnp.maximum(marks, last)
    mark = marks.astype(jnp.float32)[CHUNK - 1:CHUNK, :]
    limit = jnp.where(mark > MARK / 2, mark - MARK, float(BLOCK)).astype(jnp.int32)
    chunks = jnp.where((lane1 < 2 * blocks) & ((lane1 // per_row) % 2 == plane), (limit + (CHUNK - 1)) // CHUNK, 0)
    upto = chunks
    step = 1
    while step < 2 * blocks:
        upto = upto + jnp.where(lane1 >= step, pltpu.roll(upto, step, 1), 0)
        step *= 2
    before = upto - chunks
    square = (128, 128)
    down = jnp.broadcast_to(upto.astype(jnp.float32), square).T
    at_chunk = lax.broadcasted_iota(jnp.int32, square, 1).astype(jnp.float32)
    earlier = (down <= at_chunk) & (lax.broadcasted_iota(jnp.int32, square, 0) < 2 * blocks)
    shard = jnp.sum(earlier.astype(jnp.float32), axis=0, keepdims=True).astype(jnp.int32)
    shard = jnp.broadcast_to(jnp.minimum(shard, 2 * blocks - 1), (8, 128))
    skipped = (lane - jnp.take_along_axis(jnp.broadcast_to(before, (8, 128)), shard, axis=1)) * CHUNK
    position = place_ref[3] + shard * stride + skipped
    held = jnp.take_along_axis(jnp.broadcast_to(limit, (8, 128)), shard, axis=1) - skipped
    total = jnp.max(upto, axis=1, keepdims=True)
    held = jnp.where(lane < total, held, 0)
    length = SIDES * piece
    for y_step, ref, start in zip(STEPS, (row_ref, rest_ref, rest_ref, rest_ref), (0, 0, length, 2 * length)):
        y = (place_ref[0] + SIDES - y_step) % SIDES
        for spot, x_step in enumerate(STEPS):
            x = (place_ref[1] + SIDES - x_step) % SIDES
            to = pl.multiple_of((y * SIDES + x) * piece, piece)
            slab_ref[pl.ds(to, piece), :] = ref[start + spot * piece:start + (spot + 1) * piece, :]

    max_ref[...] = jnp.full(max_ref.shape, mask_value, jnp.float32)
    before_here = pltpu.roll(before, (128 - plane * per_row) % 128, 1)
    for block in range(blocks):
        at = before_here[0, (block // per_row) * (2 * per_row) + block % per_row]
        for part in range(PARTS):
            start = block * BLOCK + part * CHUNK
            packed_ref[pl.ds(pl.multiple_of((at + part) * CHUNK, CHUNK), CHUNK), :] = slab_ref[start:start + CHUNK, :]
    total = upto[0, 2 * blocks - 1]
    firsts = [position[0, tile * SLOTS] for tile in range(most)]
    for tile in range(most):
        first_smem[tile] = firsts[tile]

    def count(tile):
        first = first_smem[tile]
        groups = jnp.int32(0)
        for group in range(tokens // GROUP):
            groups = groups + (sorted_ref[group * GROUP] >= first).astype(jnp.int32)
        return groups

    tiles = (total + SLOTS - 1) // SLOTS
    active = jnp.int32(0)
    for tile in range(most):
        active = active + ((tile < tiles) & (sorted_ref[0] >= firsts[tile])).astype(jnp.int32)

    def push(tile):
        keys = packed_ref[pl.ds(pl.multiple_of(tile * TILE, TILE), TILE), :]
        keys = jnp.concatenate([keys, jnp.zeros_like(keys)], axis=1)
        for side in range(2):
            pltpu.matmul_push_rhs(keys, 0, side, transpose=True)

    def issue(group, pair, load=None):
        for side, acc in enumerate(pair):
            start = pl.multiple_of(group * (2 * rows) + side * rows, rows)
            left = q_ref[pl.ds(start, rows), :]
            pltpu.matmul_acc_lhs(acc, jnp.concatenate([left, left], axis=1), load)

    def finish(tile, group, pair):
        halves = []
        for side, acc in enumerate(pair):
            weights = w_ref[pl.ds(pl.multiple_of(group * (2 * rows) + side * rows, rows), rows), :]
            raw = pltpu.matmul_pop(acc)
            halves.append(
                [
                    (jnp.maximum(raw[:, part * 128:part * 128 + 128], 0.0) * weights).reshape(-1, heads // 8, 8, 128).sum(1)
                    for part in range(2)
                ]
            )
        for part in range(2):
            both = jnp.concatenate([halves[0][part], halves[1][part]], axis=0)
            score_ref[2 * tile + part, pl.ds(pl.multiple_of(group * GROUP, GROUP), GROUP), :] = both.sum(1)

    @pl.when(active > 0)
    def _():
        push(0)
        issue(0, accs[:2], 0)

        def tile_step(tile, _):
            groups = count(tile)
            odd = groups % 2
            later = jnp.minimum(tile + 1, active - 1)

            def pair_step(pair, _):
                issue(2 * pair + 1, accs[2:])
                finish(tile, 2 * pair, accs[:2])
                issue(2 * pair + 2, accs[:2])
                finish(tile, 2 * pair + 1, accs[2:])
                return 0

            lax.fori_loop(0, groups // 2 - 1 + odd, pair_step, 0)

            @pl.when(odd == 1)
            def _():
                push(later)
                finish(tile, groups - 1, accs[:2])
                issue(0, accs[:2], 0)

            @pl.when(odd == 0)
            def _():
                issue(groups - 1, accs[2:])
                push(later)
                finish(tile, groups - 2, accs[:2])
                issue(0, accs[:2], 0)
                finish(tile, groups - 1, accs[2:])

            return 0

        lax.fori_loop(0, active, tile_step, 0)
        for acc in accs[:2]:
            pltpu.matmul_pop(acc)

    def reduce_step(tile, _):
        seen = []
        for part in range(2):
            chunk = tile * SLOTS + part * 8 + lane // CHUNK
            filled = lane % CHUNK < jnp.take_along_axis(held, chunk, axis=1)
            value = jnp.take_along_axis(position, chunk, axis=1) + lane % CHUNK
            seen.append(jnp.where(filled, value, FAR)[:1])
        found = [jnp.where(seen[part] <= at_ref[...], score_ref[2 * tile + part], mask_value) for part in range(2)]
        max_ref[tile] = folded(found[0], found[1], 8, wide)
        return 0

    lax.fori_loop(0, active, reduce_step, 0)
    found = [max_ref[tile] for tile in range(most)]
    for step in (4, 2, 1):
        found = [folded(a, b, step, wide) for a, b in zip(found[::2], found[1::2])]
    pooled = None
    for part in range(PARTS):
        chunk = before + jnp.minimum(part, jnp.maximum(chunks - 1, 0))
        chunk = jnp.broadcast_to(jnp.minimum(chunk, most * SLOTS - 1), (tokens, 128))
        spot = lane_of(chunk)
        value = jnp.take_along_axis(found[0], spot, axis=1)
        if len(found) > 1:
            value = jnp.where(chunk < 128, value, jnp.take_along_axis(found[1], spot, axis=1))
        pooled = value if pooled is None else jnp.maximum(pooled, value)
    pooled_ref[...] = pooled.astype(jnp.bfloat16)


def restore(plane_ref, unsort_ref, spread_ref, near_ref, far_ref, mine_ref, theirs_ref):
    half = mine_ref.shape[0]
    lane = lax.broadcasted_iota(jnp.int32, near_ref.shape, 1)
    near = (lane // (2 * SIDES)) % 2 == plane_ref[0]
    pooled = jnp.where(near, near_ref[...].astype(jnp.float32), far_ref[...].astype(jnp.float32)).astype(jnp.bfloat16)
    ordered = jnp.dot(unsort_ref[...], pooled, preferred_element_type=jnp.float32).astype(jnp.bfloat16)
    placed = jnp.dot(ordered, spread_ref[...], preferred_element_type=jnp.float32).astype(jnp.bfloat16)
    mine_ref[...] = placed[:half]
    theirs_ref[...] = placed[half:]


def body(queries, head_weights, keys, query_pos, block_limits):
    shards = lax.axis_size("blk")
    me = lax.axis_index("blk")
    core = me % 2
    member = lax.axis_index("team")
    quarter = 2 * member + core
    count, heads, head_size = queries.shape
    tokens = 2 * count
    local_blocks = keys.shape[0] // BLOCK
    cores = [(i, i ^ 1) for i in range(shards)]
    smem = pl.BlockSpec(memory_space=pltpu.SMEM)
    vmem = pl.BlockSpec(memory_space=pltpu.VMEM)

    own = queries.reshape(count * heads, head_size)
    other = swapped(own, cores, "blk")
    other_pos = swapped(query_pos, cores, "blk")
    other_weights = swapped(head_weights, cores, "blk")

    piece_shape = jax.ShapeDtypeStruct((BLOCK, head_size), keys.dtype)
    keep, give = pl.pallas_call(
        marked,
        out_shape=(piece_shape, piece_shape),
        in_specs=[pl.BlockSpec(memory_space=pl.ANY)] * 2,
        out_specs=(vmem, vmem),
        scratch_shapes=[pltpu.SMEM(block_limits.shape, jnp.int32), pltpu.SemaphoreType.DMA((3,))],
        compiler_params=pltpu.CompilerParams(vmem_limit_bytes=4 * 2**20),
        name="marked",
    )(block_limits, keys)
    got = swapped(give, cores, "blk")
    piece = jnp.where(core == 0, jnp.stack([keep, got]), jnp.stack([got, keep]))

    def moved(y_step, z_step, x_step):
        pairs = []
        for source in range(shards):
            c, x, z, y = source % 2, source // 2 % SIDES, source // (2 * SIDES) % 2, source // (4 * SIDES)
            x, z, y = (x + x_step) % SIDES, (z + z_step) % 2, (y + y_step) % SIDES
            pairs.append((source, ((y * 2 + z) * SIDES + x) * 2 + c))
        return pairs

    piece = piece.reshape(2 * BLOCK, head_size)
    pieces = [piece] + [swapped(piece, moved(0, 0, step), "blk") for step in STEPS[1:]]

    piece, query_pos, head_weights, other_pos, other_weights = lax.optimization_barrier(
        (piece, query_pos, head_weights, other_pos, other_weights)
    )
    positions = jnp.concatenate([query_pos, other_pos])
    flat = [value.reshape(count * heads) for value in (head_weights, other_weights)]

    index = jnp.arange(tokens, dtype=jnp.int32)
    ahead = (positions[None, :] > positions[:, None]) | (
        (positions[None, :] == positions[:, None]) & (index[None, :] < index[:, None])
    )
    rank = jnp.sum(ahead.astype(jnp.int32), axis=1)
    hit = rank[None, :] == index[:, None]
    in_order = jnp.sum(jnp.where(hit, positions[None, :], 0), axis=1)
    at = jnp.broadcast_to(in_order[:, None], (tokens, 128))
    unsort = (rank[:, None] == index[None, :]).astype(jnp.bfloat16)
    pieces, rank, *flat = lax.optimization_barrier((pieces, rank, *flat))
    row = jnp.concatenate(pieces)
    row, *flat = lax.optimization_barrier((row, *flat))
    wide = [jnp.broadcast_to(value[:, None], (count * heads, 128)) for value in flat]
    lane = jnp.arange(128, dtype=jnp.int32)
    target = lane * local_blocks + quarter
    spread = ((lane < shards)[:, None] & (target[:, None] == jnp.arange(shards * local_blocks)[None, :])).astype(jnp.bfloat16)

    q_rows, w_rows = pl.pallas_call(
        lambda *refs: arrange(tokens, heads, head_size ** (-0.5), *refs),
        out_shape=(
            jax.ShapeDtypeStruct((tokens * heads, head_size), jnp.bfloat16),
            jax.ShapeDtypeStruct((tokens * heads, 128), jnp.float32),
        ),
        in_specs=[smem] + [vmem] * 4,
        out_specs=(vmem, vmem),
        compiler_params=pltpu.CompilerParams(vmem_limit_bytes=4 * 2**20),
        cost_estimate=pl.CostEstimate(flops=0, bytes_accessed=12 * 2**20, transcendentals=0),
        name="arranged",
    )(rank, own, other, *wide)

    rest = [swapped(row, moved(step, 0, 0), "blk") for step in STEPS[1:]]
    rest, q_rows, w_rows = lax.optimization_barrier((rest, q_rows, w_rows))
    rest = jnp.concatenate(rest)
    near = [row, rest]
    far = [swapped(value, moved(0, 1, 0), "blk") for value in near]

    result = jax.ShapeDtypeStruct((count, shards * local_blocks), jnp.bfloat16)
    slots = shards // 2 * PARTS
    accs = [pltpu.ACC(side)((GROUP // 2 * heads, TILE), jnp.float32) for _ in range(2) for side in range(2)]

    def kernel(*refs):
        pl.run_scoped(lambda *accs: scores(tokens, heads, local_blocks * BLOCK, *refs, *accs), *accs)

    def pooled(values, plane):
        place = jnp.stack([me // (4 * SIDES), me // 2 % SIDES, plane, quarter * BLOCK]).astype(jnp.int32)
        return pl.pallas_call(
            kernel,
            out_shape=jax.ShapeDtypeStruct((tokens, 128), jnp.bfloat16),
            in_specs=[smem] * 2 + [vmem] * 5,
            out_specs=vmem,
            scratch_shapes=[
                pltpu.VMEM((shards // 2 * BLOCK, head_size), jnp.bfloat16),
                pltpu.VMEM(((slots + PARTS) * CHUNK, head_size), jnp.bfloat16),
                    pltpu.VMEM((2 * (slots // SLOTS), tokens, 128), jnp.float32),
                pltpu.VMEM((slots // SLOTS, tokens, 128), jnp.float32),
                pltpu.SMEM((slots // SLOTS,), jnp.int32),
            ],
            compiler_params=pltpu.CompilerParams(vmem_limit_bytes=8 * 2**20),
            cost_estimate=pl.CostEstimate(flops=2**32, bytes_accessed=8 * 2**20, transcendentals=0),
            name="pooled_scores",
        )(in_order, place, q_rows, w_rows, at, *values)

    plane = me // (2 * SIDES) % 2
    mine, theirs = pl.pallas_call(
        restore,
        out_shape=(result, result),
        in_specs=[smem] + [vmem] * 4,
        out_specs=(vmem, vmem),
        compiler_params=pltpu.CompilerParams(vmem_limit_bytes=4 * 2**20),
        name="restored",
    )(plane[None].astype(jnp.int32), unsort, spread, pooled(near, plane), pooled(far, 1 - plane))
    chip = mine + swapped(theirs, cores, "blk")
    return (chip + swapped(chip, [(0, 1), (1, 0)], "team")).astype(jnp.float32)


def solution(mesh):
    in_specs = (P("blk", None, None), P("blk", None), P("blk", None), P("blk"), P("blk"))
    out_specs = P("blk", None)

    def step(*args):
        with jax.sharding.use_abstract_mesh(mesh.abstract_mesh):
            return jax.shard_map(body, mesh=mesh, in_specs=in_specs, out_specs=out_specs, check_vma=False)(*args)

    return step
```

```python
import jax
import jax.numpy as jnp
from jax import lax
from jax.experimental import pallas as pl
from jax.experimental.pallas import tpu as pltpu
from jax.sharding import PartitionSpec as P

BLOCK = 64
CHUNK = 16
GROUP = 16
TILE = 256
PARTS = BLOCK // CHUNK
SLOTS = TILE // CHUNK
MARK = 100.0
SIDES = 4
STEPS = (0, 1, 3, 2)
FAR = 1 << 30
mask_value = -8.0


def swapped(value, pairs, axis):
    return lax.ppermute(value, axis, pairs)


def marked(limit_hbm, key_hbm, keep_ref, give_ref, limit_ref, sems):
    me = lax.axis_index("blk")
    keep = 2 * lax.axis_index("team") + me % 2
    picks = ((keep_ref, keep), (give_ref, keep + 1 - 2 * (keep % 2)))
    copies = [pltpu.make_async_copy(limit_hbm, limit_ref, sems.at[2])]
    for n, (ref, block) in enumerate(picks):
        start = pl.multiple_of(block * BLOCK, BLOCK)
        copies.append(pltpu.make_async_copy(key_hbm.at[pl.ds(start, BLOCK), :], ref, sems.at[n]))
    for copy in copies:
        copy.start()
    for copy in copies:
        copy.wait()
    for ref, block in picks:
        limit = limit_ref[block]
        last = ref[BLOCK - CHUNK:, :].astype(jnp.float32)
        row = lax.broadcasted_iota(jnp.int32, last.shape, 0)
        column = lax.broadcasted_iota(jnp.int32, last.shape, 1)
        mark = jnp.where(column == me, (limit + MARK).astype(jnp.float32), 0.0)
        unfilled = jnp.where(limit < BLOCK, CHUNK - 1, CHUNK)
        ref[BLOCK - CHUNK:, :] = jnp.where(row == unfilled, mark, last).astype(ref.dtype)


def arrange(tokens, heads, scale, rank_ref, own_ref, other_ref, own_weight_ref, other_weight_ref, q_ref, w_ref):
    half = tokens // 2

    def step(token, _):
        start = pl.multiple_of(token * heads, heads)
        for ref, weight_ref, first in ((own_ref, own_weight_ref, 0), (other_ref, other_weight_ref, half)):
            to = pl.multiple_of(rank_ref[first + token] * heads, heads)
            q_ref[pl.ds(to, heads), :] = ref[pl.ds(start, heads), :]
            w_ref[pl.ds(to, heads), :] = weight_ref[pl.ds(start, heads), :] * scale
        return 0

    lax.fori_loop(0, half, step, 0, unroll=4)


def lane_of(chunk):
    return (chunk & 7) * 16 + ((chunk >> 3) & 1) * 8 + ((chunk >> 4) & 1) * 4 + ((chunk >> 5) & 1) * 2 + ((chunk >> 6) & 1)


def folded(a, b, step, lane):
    return jnp.where(
        (lane & step) == 0,
        jnp.maximum(a, pltpu.roll(a, 128 - step, 1)),
        jnp.maximum(b, pltpu.roll(b, step, 1)),
    )


def scores(tokens, heads, stride, sorted_ref, place_ref, q_ref, w_ref, at_ref, row_ref, rest_ref,
           pooled_ref, slab_ref, packed_ref, score_ref, max_ref, first_smem, *accs):
    blocks = slab_ref.shape[0] // BLOCK
    piece = 2 * BLOCK
    per_row = SIDES * 2
    most = max_ref.shape[0]
    rows = GROUP // 2 * heads
    plane = place_ref[2]
    lane1 = lax.broadcasted_iota(jnp.int32, (1, 128), 1)
    lane = lax.broadcasted_iota(jnp.int32, (8, 128), 1)
    wide = lax.broadcasted_iota(jnp.int32, (tokens, 128), 1)

    marks = None
    for ref in (row_ref, rest_ref):
        for end in range(BLOCK, ref.shape[0] + 1, BLOCK):
            last = ref[end - CHUNK:end, :]
            marks = last if marks is None else jnp.maximum(marks, last)
    mark = marks.astype(jnp.float32)[CHUNK - 1:CHUNK, :]
    limit = jnp.where(mark > MARK / 2, mark - MARK, float(BLOCK)).astype(jnp.int32)
    chunks = jnp.where((lane1 < 2 * blocks) & ((lane1 // per_row) % 2 == plane), (limit + (CHUNK - 1)) // CHUNK, 0)
    square = (128, 128)
    across_lanes = lax.broadcasted_iota(jnp.int32, square, 1)
    down_rows = lax.broadcasted_iota(jnp.int32, square, 0)
    along = jnp.broadcast_to(chunks.astype(jnp.float32), square)
    upto = jnp.sum(jnp.where(down_rows <= across_lanes, along.T, 0.0), axis=0, keepdims=True).astype(jnp.int32)
    before = upto - chunks
    down = jnp.sum(jnp.where(across_lanes <= down_rows, along, 0.0), axis=1, keepdims=True)
    earlier = (down <= across_lanes.astype(jnp.float32)) & (down_rows < 2 * blocks)
    shard = jnp.sum(earlier.astype(jnp.float32), axis=0, keepdims=True).astype(jnp.int32)
    shard = jnp.broadcast_to(jnp.minimum(shard, 2 * blocks - 1), (8, 128))
    skipped = (lane - jnp.take_along_axis(jnp.broadcast_to(before, (8, 128)), shard, axis=1)) * CHUNK
    position = place_ref[3] + shard * stride + skipped
    held = jnp.take_along_axis(jnp.broadcast_to(limit, (8, 128)), shard, axis=1) - skipped
    total = jnp.max(upto, axis=1, keepdims=True)
    held = jnp.where(lane < total, held, 0)
    length = SIDES * piece
    for y_step, ref, start in zip(STEPS, (row_ref, rest_ref, rest_ref, rest_ref), (0, 0, length, 2 * length)):
        y = (place_ref[0] + SIDES - y_step) % SIDES
        for spot, x_step in enumerate(STEPS):
            x = (place_ref[1] + SIDES - x_step) % SIDES
            to = pl.multiple_of((y * SIDES + x) * piece, piece)
            slab_ref[pl.ds(to, piece), :] = ref[start + spot * piece:start + (spot + 1) * piece, :]

    max_ref[...] = jnp.full(max_ref.shape, mask_value, jnp.float32)
    before_here = pltpu.roll(before, (128 - plane * per_row) % 128, 1)
    for block in range(blocks):
        at = before_here[0, (block // per_row) * (2 * per_row) + block % per_row]
        for part in range(PARTS):
            start = block * BLOCK + part * CHUNK
            packed_ref[pl.ds(pl.multiple_of((at + part) * CHUNK, CHUNK), CHUNK), :] = slab_ref[start:start + CHUNK, :]
    total = upto[0, 2 * blocks - 1]
    firsts = [position[0, tile * SLOTS] for tile in range(most)]
    for tile in range(most):
        first_smem[tile] = firsts[tile]

    def count(tile):
        first = first_smem[tile]
        groups = jnp.int32(0)
        for group in range(tokens // GROUP):
            groups = groups + (sorted_ref[group * GROUP] >= first).astype(jnp.int32)
        return groups

    tiles = (total + SLOTS - 1) // SLOTS
    active = jnp.int32(0)
    for tile in range(most):
        active = active + ((tile < tiles) & (sorted_ref[0] >= firsts[tile])).astype(jnp.int32)

    def push(tile):
        keys = packed_ref[pl.ds(pl.multiple_of(tile * TILE, TILE), TILE), :]
        keys = jnp.concatenate([keys, jnp.zeros_like(keys)], axis=1)
        for side in range(2):
            pltpu.matmul_push_rhs(keys, 0, side, transpose=True)

    def issue(group, pair, load=None):
        for side, acc in enumerate(pair):
            start = pl.multiple_of(group * (2 * rows) + side * rows, rows)
            left = q_ref[pl.ds(start, rows), :]
            pltpu.matmul_acc_lhs(acc, jnp.concatenate([left, left], axis=1), load)

    def finish(tile, group, pair):
        halves = []
        for side, acc in enumerate(pair):
            weights = w_ref[pl.ds(pl.multiple_of(group * (2 * rows) + side * rows, rows), rows), :]
            raw = pltpu.matmul_pop(acc)
            halves.append(
                [
                    (jnp.maximum(raw[:, part * 128:part * 128 + 128], 0.0) * weights).reshape(-1, heads // 8, 8, 128).sum(1)
                    for part in range(2)
                ]
            )
        for part in range(2):
            both = jnp.concatenate([halves[0][part], halves[1][part]], axis=0)
            score_ref[2 * tile + part, pl.ds(pl.multiple_of(group * GROUP, GROUP), GROUP), :] = both.sum(1)

    @pl.when(active > 0)
    def _():
        push(0)
        issue(0, accs[:2], 0)

        def tile_step(tile, _):
            groups = count(tile)
            odd = groups % 2
            later = jnp.minimum(tile + 1, active - 1)

            def pair_step(pair, _):
                issue(2 * pair + 1, accs[2:])
                finish(tile, 2 * pair, accs[:2])
                issue(2 * pair + 2, accs[:2])
                finish(tile, 2 * pair + 1, accs[2:])
                return 0

            lax.fori_loop(0, groups // 2 - 1 + odd, pair_step, 0)

            @pl.when(odd == 1)
            def _():
                push(later)
                finish(tile, groups - 1, accs[:2])
                issue(0, accs[:2], 0)

            @pl.when(odd == 0)
            def _():
                issue(groups - 1, accs[2:])
                push(later)
                finish(tile, groups - 2, accs[:2])
                issue(0, accs[:2], 0)
                finish(tile, groups - 1, accs[2:])

            return 0

        lax.fori_loop(0, active, tile_step, 0)
        for acc in accs[:2]:
            pltpu.matmul_pop(acc)

    def reduce_step(tile, _):
        seen = []
        for part in range(2):
            chunk = tile * SLOTS + part * 8 + lane // CHUNK
            filled = lane % CHUNK < jnp.take_along_axis(held, chunk, axis=1)
            value = jnp.take_along_axis(position, chunk, axis=1) + lane % CHUNK
            seen.append(jnp.where(filled, value, FAR)[:1])
        found = [jnp.where(seen[part] <= at_ref[...], score_ref[2 * tile + part], mask_value) for part in range(2)]
        max_ref[tile] = folded(found[0], found[1], 8, wide)
        return 0

    lax.fori_loop(0, active, reduce_step, 0)
    found = [max_ref[tile] for tile in range(most)]
    for step in (4, 2, 1):
        found = [folded(a, b, step, wide) for a, b in zip(found[::2], found[1::2])]
    pooled = None
    for part in range(PARTS):
        chunk = before + jnp.minimum(part, jnp.maximum(chunks - 1, 0))
        chunk = jnp.broadcast_to(jnp.minimum(chunk, most * SLOTS - 1), (tokens, 128))
        spot = lane_of(chunk)
        value = jnp.take_along_axis(found[0], spot, axis=1)
        if len(found) > 1:
            value = jnp.where(chunk < 128, value, jnp.take_along_axis(found[1], spot, axis=1))
        pooled = value if pooled is None else jnp.maximum(pooled, value)
    pooled_ref[...] = pooled.astype(jnp.bfloat16)


def restore(plane_ref, unsort_ref, spread_ref, near_ref, far_ref, mine_ref, theirs_ref):
    half = mine_ref.shape[0]
    lane = lax.broadcasted_iota(jnp.int32, near_ref.shape, 1)
    near = (lane // (2 * SIDES)) % 2 == plane_ref[0]
    pooled = jnp.where(near, near_ref[...].astype(jnp.float32), far_ref[...].astype(jnp.float32)).astype(jnp.bfloat16)
    ordered = jnp.dot(unsort_ref[...], pooled, preferred_element_type=jnp.float32).astype(jnp.bfloat16)
    placed = jnp.dot(ordered, spread_ref[...], preferred_element_type=jnp.float32).astype(jnp.bfloat16)
    mine_ref[...] = placed[:half]
    theirs_ref[...] = placed[half:]


def body(queries, head_weights, keys, query_pos, block_limits):
    shards = lax.axis_size("blk")
    me = lax.axis_index("blk")
    core = me % 2
    member = lax.axis_index("team")
    quarter = 2 * member + core
    count, heads, head_size = queries.shape
    tokens = 2 * count
    local_blocks = keys.shape[0] // BLOCK
    cores = [(i, i ^ 1) for i in range(shards)]
    smem = pl.BlockSpec(memory_space=pltpu.SMEM)
    vmem = pl.BlockSpec(memory_space=pltpu.VMEM)

    own = queries.reshape(count * heads, head_size)
    other = swapped(own, cores, "blk")
    other_pos = swapped(query_pos, cores, "blk")
    other_weights = swapped(head_weights, cores, "blk")

    piece_shape = jax.ShapeDtypeStruct((BLOCK, head_size), keys.dtype)
    keep, give = pl.pallas_call(
        marked,
        out_shape=(piece_shape, piece_shape),
        in_specs=[pl.BlockSpec(memory_space=pl.ANY)] * 2,
        out_specs=(vmem, vmem),
        scratch_shapes=[pltpu.SMEM(block_limits.shape, jnp.int32), pltpu.SemaphoreType.DMA((3,))],
        compiler_params=pltpu.CompilerParams(vmem_limit_bytes=4 * 2**20),
        name="marked",
    )(block_limits, keys)
    got = swapped(give, cores, "blk")
    piece = jnp.where(core == 0, jnp.stack([keep, got]), jnp.stack([got, keep]))

    def moved(y_step, z_step, x_step):
        pairs = []
        for source in range(shards):
            c, x, z, y = source % 2, source // 2 % SIDES, source // (2 * SIDES) % 2, source // (4 * SIDES)
            x, z, y = (x + x_step) % SIDES, (z + z_step) % 2, (y + y_step) % SIDES
            pairs.append((source, ((y * 2 + z) * SIDES + x) * 2 + c))
        return pairs

    piece = piece.reshape(2 * BLOCK, head_size)
    pieces = [piece] + [swapped(piece, moved(0, 0, step), "blk") for step in STEPS[1:]]

    piece, query_pos, head_weights, other_pos, other_weights = lax.optimization_barrier(
        (piece, query_pos, head_weights, other_pos, other_weights)
    )
    positions = jnp.concatenate([query_pos, other_pos])
    flat = [value.reshape(count * heads) for value in (head_weights, other_weights)]

    index = jnp.arange(tokens, dtype=jnp.int32)
    ahead = (positions[None, :] > positions[:, None]) | (
        (positions[None, :] == positions[:, None]) & (index[None, :] < index[:, None])
    )
    rank = jnp.sum(ahead.astype(jnp.int32), axis=1)
    hit = rank[None, :] == index[:, None]
    in_order = jnp.sum(jnp.where(hit, positions[None, :], 0), axis=1)
    at = jnp.broadcast_to(in_order[:, None], (tokens, 128))
    unsort = (rank[:, None] == index[None, :]).astype(jnp.bfloat16)
    pieces, rank, *flat = lax.optimization_barrier((pieces, rank, *flat))
    row = jnp.concatenate(pieces)
    row, *flat = lax.optimization_barrier((row, *flat))
    wide = [jnp.broadcast_to(value[:, None], (count * heads, 128)) for value in flat]
    lane = jnp.arange(128, dtype=jnp.int32)
    target = lane * local_blocks + quarter
    spread = ((lane < shards)[:, None] & (target[:, None] == jnp.arange(shards * local_blocks)[None, :])).astype(jnp.bfloat16)

    q_rows, w_rows = pl.pallas_call(
        lambda *refs: arrange(tokens, heads, head_size ** (-0.5), *refs),
        out_shape=(
            jax.ShapeDtypeStruct((tokens * heads, head_size), jnp.bfloat16),
            jax.ShapeDtypeStruct((tokens * heads, 128), jnp.float32),
        ),
        in_specs=[smem] + [vmem] * 4,
        out_specs=(vmem, vmem),
        compiler_params=pltpu.CompilerParams(vmem_limit_bytes=4 * 2**20),
        cost_estimate=pl.CostEstimate(flops=0, bytes_accessed=12 * 2**20, transcendentals=0),
        name="arranged",
    )(rank, own, other, *wide)

    rest = [swapped(row, moved(step, 0, 0), "blk") for step in STEPS[1:]]
    rest, q_rows, w_rows = lax.optimization_barrier((rest, q_rows, w_rows))
    rest = jnp.concatenate(rest)
    near = [row, rest]
    far = [swapped(value, moved(0, 1, 0), "blk") for value in near]

    result = jax.ShapeDtypeStruct((count, shards * local_blocks), jnp.bfloat16)
    slots = shards // 2 * PARTS
    accs = [pltpu.ACC(side)((GROUP // 2 * heads, TILE), jnp.float32) for _ in range(2) for side in range(2)]

    def kernel(*refs):
        pl.run_scoped(lambda *accs: scores(tokens, heads, local_blocks * BLOCK, *refs, *accs), *accs)

    def pooled(values, plane):
        place = jnp.stack([me // (4 * SIDES), me // 2 % SIDES, plane, quarter * BLOCK]).astype(jnp.int32)
        return pl.pallas_call(
            kernel,
            out_shape=jax.ShapeDtypeStruct((tokens, 128), jnp.bfloat16),
            in_specs=[smem] * 2 + [vmem] * 5,
            out_specs=vmem,
            scratch_shapes=[
                pltpu.VMEM((shards // 2 * BLOCK, head_size), jnp.bfloat16),
                pltpu.VMEM(((slots + PARTS) * CHUNK, head_size), jnp.bfloat16),
                    pltpu.VMEM((2 * (slots // SLOTS), tokens, 128), jnp.float32),
                pltpu.VMEM((slots // SLOTS, tokens, 128), jnp.float32),
                pltpu.SMEM((slots // SLOTS,), jnp.int32),
            ],
            compiler_params=pltpu.CompilerParams(vmem_limit_bytes=8 * 2**20),
            cost_estimate=pl.CostEstimate(flops=2**32, bytes_accessed=8 * 2**20, transcendentals=0),
            name="pooled_scores",
        )(in_order, place, q_rows, w_rows, at, *values)

    plane = me // (2 * SIDES) % 2
    mine, theirs = pl.pallas_call(
        restore,
        out_shape=(result, result),
        in_specs=[smem] + [vmem] * 4,
        out_specs=(vmem, vmem),
        compiler_params=pltpu.CompilerParams(vmem_limit_bytes=4 * 2**20),
        name="restored",
    )(plane[None].astype(jnp.int32), unsort, spread, pooled(near, plane), pooled(far, 1 - plane))
    chip = mine + swapped(theirs, cores, "blk")
    return (chip + swapped(chip, [(0, 1), (1, 0)], "team")).astype(jnp.float32)


def solution(mesh):
    in_specs = (P("blk", None, None), P("blk", None), P("blk", None), P("blk"), P("blk"))
    out_specs = P("blk", None)

    def step(*args):
        with jax.sharding.use_abstract_mesh(mesh.abstract_mesh):
            return jax.shard_map(body, mesh=mesh, in_specs=in_specs, out_specs=out_specs, check_vma=False)(*args)

    return step
```

```python
import jax
import jax.numpy as jnp
from jax import lax
from jax.experimental import pallas as pl
from jax.experimental.pallas import tpu as pltpu
from jax.sharding import PartitionSpec as P

BLOCK = 64
CHUNK = 16
GROUP = 16
TILE = 256
PARTS = BLOCK // CHUNK
SLOTS = TILE // CHUNK
MARK = 100.0
SIDES = 4
STEPS = (0, 1, 3, 2)
FAR = 1 << 30
mask_value = -8.0


def swapped(value, pairs, axis):
    return lax.ppermute(value, axis, pairs)


def marked(limit_hbm, key_hbm, keep_ref, give_ref, limit_ref, sems):
    me = lax.axis_index("blk")
    keep = 2 * lax.axis_index("team") + me % 2
    picks = ((keep_ref, keep), (give_ref, keep + 1 - 2 * (keep % 2)))
    copies = [pltpu.make_async_copy(limit_hbm, limit_ref, sems.at[2])]
    for n, (ref, block) in enumerate(picks):
        start = pl.multiple_of(block * BLOCK, BLOCK)
        copies.append(pltpu.make_async_copy(key_hbm.at[pl.ds(start, BLOCK), :], ref, sems.at[n]))
    for copy in copies:
        copy.start()
    for copy in copies:
        copy.wait()
    for ref, block in picks:
        limit = limit_ref[block]
        last = ref[BLOCK - CHUNK:, :].astype(jnp.float32)
        row = lax.broadcasted_iota(jnp.int32, last.shape, 0)
        column = lax.broadcasted_iota(jnp.int32, last.shape, 1)
        mark = jnp.where(column == me, (limit + MARK).astype(jnp.float32), 0.0)
        unfilled = jnp.where(limit < BLOCK, CHUNK - 1, CHUNK)
        ref[BLOCK - CHUNK:, :] = jnp.where(row == unfilled, mark, last).astype(ref.dtype)


def arrange(tokens, heads, rank_ref, own_ref, other_ref, own_weight_ref, other_weight_ref, q_ref, w_ref):
    half = tokens // 2

    def step(token, _):
        start = pl.multiple_of(token * heads, heads)
        for ref, weight_ref, first in ((own_ref, own_weight_ref, 0), (other_ref, other_weight_ref, half)):
            to = pl.multiple_of(rank_ref[first + token] * heads, heads)
            q_ref[pl.ds(to, heads), :] = ref[pl.ds(start, heads), :]
            w_ref[pl.ds(to, heads), :] = weight_ref[pl.ds(start, heads), :]
        return 0

    lax.fori_loop(0, half, step, 0, unroll=4)


def lane_of(chunk):
    return (chunk & 7) * 16 + ((chunk >> 3) & 1) * 8 + ((chunk >> 4) & 1) * 4 + ((chunk >> 5) & 1) * 2 + ((chunk >> 6) & 1)


def folded(a, b, step, lane):
    return jnp.where(
        (lane & step) == 0,
        jnp.maximum(a, pltpu.roll(a, 128 - step, 1)),
        jnp.maximum(b, pltpu.roll(b, step, 1)),
    )


def scores(tokens, heads, stride, sorted_ref, place_ref, q_ref, w_ref, at_ref, row_ref, rest_ref,
           pooled_ref, slab_ref, packed_ref, score_ref, max_ref, first_smem, *accs):
    blocks = slab_ref.shape[0] // BLOCK
    piece = 2 * BLOCK
    per_row = SIDES * 2
    most = max_ref.shape[0]
    rows = GROUP // 2 * heads
    plane = place_ref[2]
    scale = q_ref.shape[1] ** (-0.5)
    lane1 = lax.broadcasted_iota(jnp.int32, (1, 128), 1)
    lane = lax.broadcasted_iota(jnp.int32, (8, 128), 1)
    wide = lax.broadcasted_iota(jnp.int32, (tokens, 128), 1)

    marks = None
    for ref in (row_ref, rest_ref):
        for end in range(BLOCK, ref.shape[0] + 1, BLOCK):
            last = ref[end - CHUNK:end, :]
            marks = last if marks is None else jnp.maximum(marks, last)
    mark = marks.astype(jnp.float32)[CHUNK - 1:CHUNK, :]
    limit = jnp.where(mark > MARK / 2, mark - MARK, float(BLOCK)).astype(jnp.int32)
    chunks = jnp.where((lane1 < 2 * blocks) & ((lane1 // per_row) % 2 == plane), (limit + (CHUNK - 1)) // CHUNK, 0)
    square = (128, 128)
    across_lanes = lax.broadcasted_iota(jnp.int32, square, 1)
    down_rows = lax.broadcasted_iota(jnp.int32, square, 0)
    along = jnp.broadcast_to(chunks.astype(jnp.float32), square)
    upto = jnp.sum(jnp.where(down_rows <= across_lanes, along.T, 0.0), axis=0, keepdims=True).astype(jnp.int32)
    before = upto - chunks
    down = jnp.sum(jnp.where(across_lanes <= down_rows, along, 0.0), axis=1, keepdims=True)
    earlier = (down <= across_lanes.astype(jnp.float32)) & (down_rows < 2 * blocks)
    shard = jnp.sum(earlier.astype(jnp.float32), axis=0, keepdims=True).astype(jnp.int32)
    shard = jnp.broadcast_to(jnp.minimum(shard, 2 * blocks - 1), (8, 128))
    skipped = (lane - jnp.take_along_axis(jnp.broadcast_to(before, (8, 128)), shard, axis=1)) * CHUNK
    position = place_ref[3] + shard * stride + skipped
    held = jnp.take_along_axis(jnp.broadcast_to(limit, (8, 128)), shard, axis=1) - skipped
    total = jnp.max(upto, axis=1, keepdims=True)
    held = jnp.where(lane < total, held, 0)
    length = SIDES * piece
    for y_step, ref, start in zip(STEPS, (row_ref, rest_ref, rest_ref, rest_ref), (0, 0, length, 2 * length)):
        y = (place_ref[0] + SIDES - y_step) % SIDES
        for spot, x_step in enumerate(STEPS):
            x = (place_ref[1] + SIDES - x_step) % SIDES
            to = pl.multiple_of((y * SIDES + x) * piece, piece)
            slab_ref[pl.ds(to, piece), :] = ref[start + spot * piece:start + (spot + 1) * piece, :]

    max_ref[...] = jnp.full(max_ref.shape, mask_value, jnp.float32)
    before_here = pltpu.roll(before, (128 - plane * per_row) % 128, 1)
    for block in range(blocks):
        at = before_here[0, (block // per_row) * (2 * per_row) + block % per_row]
        for part in range(PARTS):
            start = block * BLOCK + part * CHUNK
            packed_ref[pl.ds(pl.multiple_of((at + part) * CHUNK, CHUNK), CHUNK), :] = slab_ref[start:start + CHUNK, :]
    total = upto[0, 2 * blocks - 1]
    firsts = [position[0, tile * SLOTS] for tile in range(most)]
    for tile in range(most):
        first_smem[tile] = firsts[tile]

    def count(tile):
        first = first_smem[tile]
        groups = jnp.int32(0)
        for group in range(tokens // GROUP):
            groups = groups + (sorted_ref[group * GROUP] >= first).astype(jnp.int32)
        return groups

    tiles = (total + SLOTS - 1) // SLOTS
    active = jnp.int32(0)
    for tile in range(most):
        active = active + ((tile < tiles) & (sorted_ref[0] >= firsts[tile])).astype(jnp.int32)

    def push(tile):
        keys = packed_ref[pl.ds(pl.multiple_of(tile * TILE, TILE), TILE), :]
        keys = jnp.concatenate([keys, jnp.zeros_like(keys)], axis=1)
        for side in range(2):
            pltpu.matmul_push_rhs(keys, 0, side, transpose=True)

    def issue(group, pair, load=None):
        for side, acc in enumerate(pair):
            start = pl.multiple_of(group * (2 * rows) + side * rows, rows)
            left = q_ref[pl.ds(start, rows), :]
            pltpu.matmul_acc_lhs(acc, jnp.concatenate([left, left], axis=1), load)

    def finish(tile, group, pair):
        halves = []
        for side, acc in enumerate(pair):
            weights = w_ref[pl.ds(pl.multiple_of(group * (2 * rows) + side * rows, rows), rows), :]
            raw = pltpu.matmul_pop(acc)
            halves.append(
                [
                    (jnp.maximum(raw[:, part * 128:part * 128 + 128], 0.0) * weights).reshape(-1, heads // 8, 8, 128).sum(1)
                    for part in range(2)
                ]
            )
        for part in range(2):
            both = jnp.concatenate([halves[0][part], halves[1][part]], axis=0)
            score_ref[2 * tile + part, pl.ds(pl.multiple_of(group * GROUP, GROUP), GROUP), :] = both.sum(1)

    @pl.when(active > 0)
    def _():
        push(0)
        issue(0, accs[:2], 0)

        def tile_step(tile, _):
            groups = count(tile)
            odd = groups % 2
            later = jnp.minimum(tile + 1, active - 1)

            def pair_step(pair, _):
                issue(2 * pair + 1, accs[2:])
                finish(tile, 2 * pair, accs[:2])
                issue(2 * pair + 2, accs[:2])
                finish(tile, 2 * pair + 1, accs[2:])
                return 0

            lax.fori_loop(0, groups // 2 - 1 + odd, pair_step, 0)

            @pl.when(odd == 1)
            def _():
                push(later)
                finish(tile, groups - 1, accs[:2])
                issue(0, accs[:2], 0)

            @pl.when(odd == 0)
            def _():
                issue(groups - 1, accs[2:])
                push(later)
                finish(tile, groups - 2, accs[:2])
                issue(0, accs[:2], 0)
                finish(tile, groups - 1, accs[2:])

            return 0

        lax.fori_loop(0, active, tile_step, 0)
        for acc in accs[:2]:
            pltpu.matmul_pop(acc)

    def reduce_step(tile, _):
        seen = []
        for part in range(2):
            chunk = tile * SLOTS + part * 8 + lane // CHUNK
            filled = lane % CHUNK < jnp.take_along_axis(held, chunk, axis=1)
            value = jnp.take_along_axis(position, chunk, axis=1) + lane % CHUNK
            seen.append(jnp.where(filled, value, FAR)[:1])
        found = [jnp.where(seen[part] <= at_ref[...], score_ref[2 * tile + part] * scale, mask_value) for part in range(2)]
        max_ref[tile] = folded(found[0], found[1], 8, wide)
        return 0

    lax.fori_loop(0, active, reduce_step, 0)
    found = [max_ref[tile] for tile in range(most)]
    for step in (4, 2, 1):
        found = [folded(a, b, step, wide) for a, b in zip(found[::2], found[1::2])]
    pooled = None
    for part in range(PARTS):
        chunk = before + jnp.minimum(part, jnp.maximum(chunks - 1, 0))
        chunk = jnp.broadcast_to(jnp.minimum(chunk, most * SLOTS - 1), (tokens, 128))
        spot = lane_of(chunk)
        value = jnp.take_along_axis(found[0], spot, axis=1)
        if len(found) > 1:
            value = jnp.where(chunk < 128, value, jnp.take_along_axis(found[1], spot, axis=1))
        pooled = value if pooled is None else jnp.maximum(pooled, value)
    pooled_ref[...] = pooled.astype(jnp.bfloat16)


def restore(plane_ref, unsort_ref, spread_ref, near_ref, far_ref, mine_ref, theirs_ref):
    half = mine_ref.shape[0]
    lane = lax.broadcasted_iota(jnp.int32, near_ref.shape, 1)
    near = (lane // (2 * SIDES)) % 2 == plane_ref[0]
    pooled = jnp.where(near, near_ref[...].astype(jnp.float32), far_ref[...].astype(jnp.float32)).astype(jnp.bfloat16)
    ordered = jnp.dot(unsort_ref[...], pooled, preferred_element_type=jnp.float32).astype(jnp.bfloat16)
    placed = jnp.dot(ordered, spread_ref[...], preferred_element_type=jnp.float32).astype(jnp.bfloat16)
    mine_ref[...] = placed[:half]
    theirs_ref[...] = placed[half:]


def body(queries, head_weights, keys, query_pos, block_limits):
    shards = lax.axis_size("blk")
    me = lax.axis_index("blk")
    core = me % 2
    member = lax.axis_index("team")
    quarter = 2 * member + core
    count, heads, head_size = queries.shape
    tokens = 2 * count
    local_blocks = keys.shape[0] // BLOCK
    cores = [(i, i ^ 1) for i in range(shards)]
    smem = pl.BlockSpec(memory_space=pltpu.SMEM)
    vmem = pl.BlockSpec(memory_space=pltpu.VMEM)

    own = queries.reshape(count * heads, head_size)
    other = swapped(own, cores, "blk")
    other_pos = swapped(query_pos, cores, "blk")
    other_weights = swapped(head_weights, cores, "blk")

    piece_shape = jax.ShapeDtypeStruct((BLOCK, head_size), keys.dtype)
    keep, give = pl.pallas_call(
        marked,
        out_shape=(piece_shape, piece_shape),
        in_specs=[pl.BlockSpec(memory_space=pl.ANY)] * 2,
        out_specs=(vmem, vmem),
        scratch_shapes=[pltpu.SMEM(block_limits.shape, jnp.int32), pltpu.SemaphoreType.DMA((3,))],
        compiler_params=pltpu.CompilerParams(vmem_limit_bytes=4 * 2**20),
        name="marked",
    )(block_limits, keys)
    got = swapped(give, cores, "blk")
    piece = jnp.where(core == 0, jnp.stack([keep, got]), jnp.stack([got, keep]))

    def moved(y_step, z_step, x_step):
        pairs = []
        for source in range(shards):
            c, x, z, y = source % 2, source // 2 % SIDES, source // (2 * SIDES) % 2, source // (4 * SIDES)
            x, z, y = (x + x_step) % SIDES, (z + z_step) % 2, (y + y_step) % SIDES
            pairs.append((source, ((y * 2 + z) * SIDES + x) * 2 + c))
        return pairs

    piece = piece.reshape(2 * BLOCK, head_size)
    pieces = [piece] + [swapped(piece, moved(0, 0, step), "blk") for step in STEPS[1:]]

    piece, query_pos, head_weights, other_pos, other_weights = lax.optimization_barrier(
        (piece, query_pos, head_weights, other_pos, other_weights)
    )
    positions = jnp.concatenate([query_pos, other_pos])
    flat = [value.reshape(count * heads) for value in (head_weights, other_weights)]

    index = jnp.arange(tokens, dtype=jnp.int32)
    ahead = (positions[None, :] > positions[:, None]) | (
        (positions[None, :] == positions[:, None]) & (index[None, :] < index[:, None])
    )
    rank = jnp.sum(ahead.astype(jnp.int32), axis=1)
    hit = rank[None, :] == index[:, None]
    in_order = jnp.sum(jnp.where(hit, positions[None, :], 0), axis=1)
    at = jnp.broadcast_to(in_order[:, None], (tokens, 128))
    unsort = (rank[:, None] == index[None, :]).astype(jnp.bfloat16)
    pieces, rank, *flat = lax.optimization_barrier((pieces, rank, *flat))
    row = jnp.concatenate(pieces)
    row, *flat = lax.optimization_barrier((row, *flat))
    wide = [jnp.broadcast_to(value[:, None], (count * heads, 128)) for value in flat]
    lane = jnp.arange(128, dtype=jnp.int32)
    target = lane * local_blocks + quarter
    spread = ((lane < shards)[:, None] & (target[:, None] == jnp.arange(shards * local_blocks)[None, :])).astype(jnp.bfloat16)

    q_rows, w_rows = pl.pallas_call(
        lambda *refs: arrange(tokens, heads, *refs),
        out_shape=(
            jax.ShapeDtypeStruct((tokens * heads, head_size), jnp.bfloat16),
            jax.ShapeDtypeStruct((tokens * heads, 128), jnp.float32),
        ),
        in_specs=[smem] + [vmem] * 4,
        out_specs=(vmem, vmem),
        compiler_params=pltpu.CompilerParams(vmem_limit_bytes=4 * 2**20),
        cost_estimate=pl.CostEstimate(flops=0, bytes_accessed=12 * 2**20, transcendentals=0),
        name="arranged",
    )(rank, own, other, *wide)

    rest = [swapped(row, moved(step, 0, 0), "blk") for step in STEPS[1:]]
    rest, q_rows, w_rows = lax.optimization_barrier((rest, q_rows, w_rows))
    rest = jnp.concatenate(rest)
    near = [row, rest]
    far = [swapped(value, moved(0, 1, 0), "blk") for value in near]

    result = jax.ShapeDtypeStruct((count, shards * local_blocks), jnp.bfloat16)
    slots = shards // 2 * PARTS
    accs = [pltpu.ACC(side)((GROUP // 2 * heads, TILE), jnp.float32) for _ in range(2) for side in range(2)]

    def kernel(*refs):
        pl.run_scoped(lambda *accs: scores(tokens, heads, local_blocks * BLOCK, *refs, *accs), *accs)

    def pooled(values, plane):
        place = jnp.stack([me // (4 * SIDES), me // 2 % SIDES, plane, quarter * BLOCK]).astype(jnp.int32)
        return pl.pallas_call(
            kernel,
            out_shape=jax.ShapeDtypeStruct((tokens, 128), jnp.bfloat16),
            in_specs=[smem] * 2 + [vmem] * 5,
            out_specs=vmem,
            scratch_shapes=[
                pltpu.VMEM((shards // 2 * BLOCK, head_size), jnp.bfloat16),
                pltpu.VMEM(((slots + PARTS) * CHUNK, head_size), jnp.bfloat16),
                    pltpu.VMEM((2 * (slots // SLOTS), tokens, 128), jnp.float32),
                pltpu.VMEM((slots // SLOTS, tokens, 128), jnp.float32),
                pltpu.SMEM((slots // SLOTS,), jnp.int32),
            ],
            compiler_params=pltpu.CompilerParams(vmem_limit_bytes=8 * 2**20),
            cost_estimate=pl.CostEstimate(flops=2**32, bytes_accessed=8 * 2**20, transcendentals=0),
            name="pooled_scores",
        )(in_order, place, q_rows, w_rows, at, *values)

    plane = me // (2 * SIDES) % 2
    mine, theirs = pl.pallas_call(
        restore,
        out_shape=(result, result),
        in_specs=[smem] + [vmem] * 4,
        out_specs=(vmem, vmem),
        compiler_params=pltpu.CompilerParams(vmem_limit_bytes=4 * 2**20),
        name="restored",
    )(plane[None].astype(jnp.int32), unsort, spread, pooled(near, plane), pooled(far, 1 - plane))
    chip = mine + swapped(theirs, cores, "blk")
    return (chip + swapped(chip, [(0, 1), (1, 0)], "team")).astype(jnp.float32)


def solution(mesh):
    in_specs = (P("blk", None, None), P("blk", None), P("blk", None), P("blk"), P("blk"))
    out_specs = P("blk", None)

    def step(*args):
        with jax.sharding.use_abstract_mesh(mesh.abstract_mesh):
            return jax.shard_map(body, mesh=mesh, in_specs=in_specs, out_specs=out_specs, check_vma=False)(*args)

    return step
```
